32 devices in a mesh: sample: 4 (over x, core), gene: 2 (over y), cohort: 4 (over z).
Axes of the slice: x: 2, y: 2, z: 4, core: 2. Of those that a mesh axis runs over, the one named last changes fastest.
Arguments:
- dosage: bfloat16 [8192, 16384], P(('sample', 'cohort'), 'gene'), may hold values from 0 to 2
- covariates: bfloat16 [8192, 32], P(('sample', 'cohort')), may hold values from 0 to 2
- phenotype: bfloat16 [8192], P(('sample', 'cohort')), may hold values from -6 to 6
- sample_mask: int32 [8192], P(('sample', 'cohort')), may hold values 0 or 1
- variant_weight: float32 [16384], replicated, may hold values from 0.1 to 1
- bucket_owner: int32 [128], replicated, may hold values from 0 to 7, as said below
- variant_gene: int32 [16384], replicated, may hold values from -1 to 63, as said below
Outputs:
- gram_tiles: float32 [8, 16, 128, 128], P(('gene', 'cohort'), 'sample')
- rho_stats: float32 [8, 64], P(None, ('gene', 'cohort'))
- gene_trace: float32 [64], P(('gene', 'cohort'))
The draws below stay inside these ranges and needn't reach their ends.
Inputs may be any that keep to these rules, and one draw needn't show every extreme that they name: `bucket_owner`: every owner holds exactly 16 buckets, at most 8 of them among the 64 buckets of one index of gene, and some owner exactly 8; of the buckets of one index of gene, exactly 16 belong to owners whose index leaves a given remainder on division by the size of the cohort axis. `variant_gene`: genes o * 8 to (o + 1) * 8 - 1 lie in the buckets of owner o, each in one or more whole buckets that are consecutive among that owner's buckets; all its buckets are full but its last, whose first 10 to 128 columns are live and the rest -1.
All inputs are finite; a program needn't handle non-finite values. No bound on the sum of `sample_mask` on one device may be relied on, other than what follows from the above.
Results may differ from the reference program's by a relative error of at most 0.0003.
Values may be sent and summed in bfloat16 or wider, within the bound.
A program may use at most 128 MiB of HBM per device.

```python
import math
import jax
import jax.numpy as jnp
from jax import lax

B_DEV = 16
COVS = 32
BUCKET_WIDTH = 128
CAP = 8
GENES_OWN = 8
OWNERS = 8
SRC_BUCKETS = 64
BUCKETS = 128
VARIANTS = 16384
GENES = 64
SAMPLES = 8192
N_GENE = 2
N_COHORT = 4


def bucket_layout(key):
    subkeys = jax.random.split(jax.random.fold_in(key, 11), 5)
    rotation = jax.random.randint(subkeys[0], (), 0, N_GENE).astype(jnp.int32)
    owner_ids = jnp.arange(OWNERS, dtype=jnp.int32)
    surplus_at = (owner_ids // N_COHORT + owner_ids % N_COHORT + rotation) % N_GENE
    deficit_at = (surplus_at + 1) % N_GENE
    mean_take = B_DEV // N_GENE
    extra_take = CAP - mean_take
    gene_ids = jnp.arange(N_GENE, dtype=jnp.int32)
    counts = mean_take + extra_take * ((gene_ids[None, :] == surplus_at[:, None]).astype(jnp.int32) - (gene_ids[None, :] == deficit_at[:, None]).astype(jnp.int32))
    running = jnp.cumsum(counts, axis=0)
    position = jnp.arange(SRC_BUCKETS, dtype=jnp.int32)
    labels = jnp.sum((running[:, None, :] <= position[None, :, None]).astype(jnp.int32), axis=0)

    def shuffle_block(block_key, column):
        return jax.random.permutation(block_key, column)
    blocks = jax.vmap(shuffle_block)(jax.random.split(subkeys[1], N_GENE), labels.T)
    owners = blocks.reshape(BUCKETS).astype(jnp.int32)
    onehot = (owners[:, None] == owner_ids[None, :]).astype(jnp.int32)
    owner_rank = jnp.sum((jnp.cumsum(onehot, axis=0) - onehot) * onehot, axis=1)

    def cut_one(cut_key):
        return jnp.sort(jax.random.permutation(cut_key, B_DEV - 1)[:GENES_OWN - 1]) + 1
    cuts = jax.vmap(cut_one)(jax.random.split(subkeys[3], OWNERS)).astype(jnp.int32)
    own_cuts = cuts[owners]
    local_gene = jnp.sum((own_cuts <= owner_rank[:, None]).astype(jnp.int32), axis=1)
    is_last = (owner_rank == B_DEV - 1) | jnp.any(own_cuts == owner_rank[:, None] + 1, axis=1)
    filled = jnp.where(is_last, jax.random.randint(subkeys[4], (BUCKETS,), 10, BUCKET_WIDTH + 1), BUCKET_WIDTH)
    column = jnp.arange(BUCKET_WIDTH, dtype=jnp.int32)
    gene_of = jnp.where(column[None, :] < filled[:, None], (owners * GENES_OWN + local_gene)[:, None], -1)
    return (owners, gene_of.reshape(VARIANTS).astype(jnp.int32))


def draw_bucket_owner(key, part):
    return bucket_layout(key)[0]


def draw_variant_gene(key, part):
    return bucket_layout(key)[1]


def draw_dosage(key, part):
    uniform_base = jax.random.uniform(key, (SAMPLES, VARIANTS + 1), jnp.float32, -1.0, 1.0)
    return (1.0 + 0.6 * uniform_base[:, 1:] + 0.4 * uniform_base[:, :-1]).astype(jnp.bfloat16)


def plant(result, stream_key, least, largest):
    extent = result.shape
    index_at = [jax.random.randint(jax.random.fold_in(stream_key, axis), (), 0, extent[axis]) for axis in range(len(extent))]
    result = result.at[tuple(index_at)].set(least)
    longest = extent.index(max(extent))
    index_at[longest] = (index_at[longest] + 1) % extent[longest]
    return result.at[tuple(index_at)].set(largest)


def shard_levels(stream_key, shape, pieces, smallest, largest):
    gain, own = 1.0, jax.random.fold_in(stream_key, 6)
    for axis_at, shards_of in pieces:
        heights = jnp.exp(jax.random.uniform(jax.random.fold_in(own, axis_at), (shards_of,), jnp.float32, smallest / len(pieces), largest / len(pieces)))
        gain = gain * jnp.repeat(heights, shape[axis_at] // shards_of).reshape([-1 if axis == axis_at else 1 for axis in range(len(shape))])
    return gain


def noise(rng, dims, width, bound, shards=(), kind=jnp.bfloat16):
    result = width * jax.random.normal(rng, dims, jnp.float32)
    if shards:
        result = result * shard_levels(rng, dims, shards, -0.22, 0.18)
    return jnp.clip(result, -bound, bound).astype(kind)


def setup_inputs(seed: int = 0) -> dict:
    streams_of = jax.random.split(jax.random.key(seed), 8)
    return {
        "dosage": draw_dosage(jax.random.fold_in(streams_of[7], 71), 0),
        "covariates": jnp.clip(2.0 * jax.random.uniform(streams_of[1], (SAMPLES, COVS), jnp.float32) ** shard_levels(streams_of[1], (SAMPLES, COVS), ((0, 16),), -0.2, 0.2), 0.0, 2.0).astype(jnp.bfloat16),
        "phenotype": noise(streams_of[2], (SAMPLES,), 1.0, 6.0, ((0, 16),)),
        "sample_mask": plant((jax.random.randint(streams_of[3], (SAMPLES,), 0, 10) < 9).astype(jnp.int32), jax.random.fold_in(streams_of[3], 1), 0, 1),
        "variant_weight": jnp.clip(jnp.exp(jax.random.uniform(streams_of[4], (VARIANTS,), jnp.float32, math.log(0.1), math.log(1.0))), 0.1, 1.0),
        "bucket_owner": draw_bucket_owner(jax.random.fold_in(streams_of[7], 71), 0),
        "variant_gene": draw_variant_gene(jax.random.fold_in(streams_of[7], 71), 0),
    }


RHO_GRID = (0.0, 0.01, 0.04, 0.09, 0.16, 0.25, 0.5, 1.0)

def solve_moments(factor, rhs):
    half = lax.linalg.triangular_solve(factor, rhs, left_side=True, lower=True)
    return lax.linalg.triangular_solve(factor, half, left_side=True, lower=True, transpose_a=True)

def segment_total(values, segment_ids):
    return jax.ops.segment_sum(values, segment_ids, num_segments=GENES + 1)[:GENES]

def reference(dosage, covariates, phenotype, sample_mask, variant_weight, bucket_owner, variant_gene):
    sample_keep = sample_mask.astype(jnp.bfloat16)
    masked_cov = covariates * sample_keep[:, None]
    left_cols = jnp.concatenate([masked_cov, (phenotype * sample_keep)[:, None]], axis=1)
    moments = jnp.dot(masked_cov.T.astype(jnp.float32), jnp.concatenate([covariates, phenotype[:, None]], axis=1).astype(jnp.float32), preferred_element_type=jnp.float32)
    factor = jnp.linalg.cholesky(moments[:, :COVS])
    beta_hat = solve_moments(factor, moments[:, COVS:])[:, 0]

    def bucket_terms(bucket):
        panel_block = lax.dynamic_slice_in_dim(dosage, bucket * BUCKET_WIDTH, BUCKET_WIDTH, 1)
        masked_block = panel_block * sample_keep[:, None]
        gram_part = jnp.dot(masked_block.T.astype(jnp.float32), panel_block.astype(jnp.float32), preferred_element_type=jnp.float32)
        cross_part = jnp.dot(left_cols.T.astype(jnp.float32), panel_block.astype(jnp.float32), preferred_element_type=jnp.float32)
        return (gram_part, cross_part)
    gram_all, cross_all = lax.map(bucket_terms, jnp.arange(BUCKETS, dtype=jnp.int32))
    cov_cross = cross_all[:, :COVS, :]
    raw_score = cross_all[:, COVS, :]
    stacked = jnp.transpose(cov_cross, (1, 0, 2)).reshape(COVS, BUCKETS * BUCKET_WIDTH)
    solved = solve_moments(factor, stacked).reshape(COVS, BUCKETS, BUCKET_WIDTH)
    projected = jnp.einsum('bcj,cbk->bjk', cov_cross, solved, precision=lax.Precision.HIGHEST)
    scores = raw_score - jnp.einsum('bcj,c->bj', cov_cross, beta_hat, precision=lax.Precision.HIGHEST)
    live_weight = jnp.where(variant_gene >= 0, variant_weight, 0.0).reshape(BUCKETS, BUCKET_WIDTH)
    tile_all = live_weight[:, :, None] * live_weight[:, None, :] * (gram_all - projected) / SAMPLES
    zscore = (live_weight * scores / math.sqrt(SAMPLES)).reshape(VARIANTS)
    segment_ids = jnp.where(variant_gene >= 0, variant_gene, GENES)
    squares = segment_total(zscore * zscore, segment_ids)
    burden_sum = segment_total(zscore, segment_ids)
    trace_sum = segment_total(jnp.diagonal(tile_all, axis1=1, axis2=2).reshape(VARIANTS), segment_ids)
    rho_col = jnp.array(RHO_GRID, dtype=jnp.float32)[:, None]
    rho_stats = ((1.0 - rho_col) * squares[None, :] + rho_col * (burden_sum * burden_sum)[None, :]) / BUCKET_WIDTH
    gene_trace = trace_sum / BUCKET_WIDTH
    onehot = (bucket_owner[:, None] == jnp.arange(OWNERS, dtype=jnp.int32)[None, :]).astype(jnp.int32)
    owner_rank = lax.optimization_barrier(jnp.sum((jnp.cumsum(onehot, axis=0) - onehot) * onehot, axis=1))
    slot_order = jnp.zeros((BUCKETS,), jnp.int32).at[bucket_owner * B_DEV + owner_rank].set(jnp.arange(BUCKETS, dtype=jnp.int32))
    gram_tiles = tile_all[slot_order].reshape(OWNERS, B_DEV, BUCKET_WIDTH, BUCKET_WIDTH)
    return (gram_tiles, rho_stats, gene_trace)
```

```python
import functools
import math

import jax
import jax.numpy as jnp
from jax import lax
from jax.experimental import pallas as pl
from jax.experimental.pallas import tpu as pltpu
from jax.sharding import PartitionSpec as P

BUCKET_WIDTH = 128
GENES_OWN = 8


RHO_GRID = (0.0, 0.01, 0.04, 0.09, 0.16, 0.25, 0.5, 1.0)


def solve_moments(factor, rhs):
    half = lax.linalg.triangular_solve(factor, rhs, left_side=True, lower=True)
    return lax.linalg.triangular_solve(factor, half, left_side=True, lower=True, transpose_a=True)


def inner_rows(first, second):
    return lax.dot_general(
        first, second, (((0,), (0,)), ((), ())), preferred_element_type=jnp.float32
    )


def block_rank(labels, group_count, label_count):
    onehot = (labels[:, None] == jnp.arange(label_count, dtype=jnp.int32)[None, :]).astype(
        jnp.int32
    )
    blocks = onehot.reshape(group_count, labels.shape[0] // group_count, label_count)
    return jnp.sum((jnp.cumsum(blocks, axis=1) - blocks) * blocks, axis=2).reshape(labels.shape[0])


def finish_slots(
    gram, cross, slot_bucket, moments, variant_weight, variant_gene, owner_here, sample_total
):
    cov_count = moments.shape[0]
    slot_count = gram.shape[0]
    span_width = gram.shape[1]
    factor = jnp.linalg.cholesky(moments[:, :cov_count])
    beta_hat = solve_moments(factor, moments[:, cov_count:])[:, 0]
    cov_cross = cross[:, :cov_count, :]
    raw_score = cross[:, cov_count, :]
    stacked = jnp.transpose(cov_cross, (1, 0, 2)).reshape(cov_count, slot_count * span_width)
    solved = solve_moments(factor, stacked).reshape(cov_count, slot_count, span_width)
    projected = jnp.einsum("bcj,cbk->bjk", cov_cross, solved, precision=lax.Precision.HIGHEST)
    scores = raw_score - jnp.einsum(
        "bcj,c->bj", cov_cross, beta_hat, precision=lax.Precision.HIGHEST
    )
    bucket_total = variant_gene.shape[0] // span_width
    weight_rows = jnp.where(variant_gene >= 0, variant_weight, 0.0).reshape(
        bucket_total, span_width
    )
    live_weight = jnp.take(weight_rows, slot_bucket, axis=0)
    tiles = live_weight[:, :, None] * live_weight[:, None, :] * (gram - projected) / sample_total
    zscore = (live_weight * scores / math.sqrt(sample_total)).reshape(slot_count * span_width)
    gene_rows = (
        jnp.take(variant_gene.reshape(bucket_total, span_width), slot_bucket, axis=0)
        - owner_here * GENES_OWN
    )
    member = (
        gene_rows.reshape(slot_count * span_width)[:, None]
        == jnp.arange(GENES_OWN, dtype=jnp.int32)[None, :]
    ).astype(jnp.float32)
    squares = jnp.dot(zscore * zscore, member, precision=lax.Precision.HIGHEST)
    burden_sum = jnp.dot(zscore, member, precision=lax.Precision.HIGHEST)
    diagonal = jnp.diagonal(tiles, axis1=1, axis2=2).reshape(slot_count * span_width)
    trace_sum = jnp.dot(diagonal, member, precision=lax.Precision.HIGHEST)
    return (tiles, squares, burden_sum, trace_sum)


def shards(dosage, covariates, phenotype, sample_mask, variant_weight, bucket_owner, variant_gene):
    gene_count = lax.axis_size("gene")
    cohort_count = lax.axis_size("cohort")
    sample_count = lax.axis_size("sample")
    owner_count = gene_count * cohort_count
    span_width = BUCKET_WIDTH
    sample_rows = dosage.shape[0]
    src_buckets = dosage.shape[1] // span_width
    total_buckets = bucket_owner.shape[0]
    held_slots = total_buckets // owner_count
    cap_slots = held_slots // 2
    share = held_slots // sample_count
    sample_total = sample_rows * sample_count * cohort_count
    cohort_here = lax.axis_index("cohort")
    owner_here = lax.axis_index("gene") * cohort_count + cohort_here
    sample_keep = sample_mask.astype(jnp.bfloat16)
    masked_cov = covariates * sample_keep[:, None]
    left_cols = jnp.concatenate([masked_cov, (phenotype * sample_keep)[:, None]], axis=1)
    moments = lax.psum(
        inner_rows(masked_cov, jnp.concatenate([covariates, phenotype[:, None]], axis=1)),
        ("sample", "cohort"),
    )
    masked_dosage = (dosage * sample_keep[:, None]).reshape(sample_rows, src_buckets, span_width)
    owner_ids = jnp.arange(owner_count, dtype=jnp.int32)
    onehot = (bucket_owner[:, None] == owner_ids[None, :]).astype(jnp.int32)
    owner_rank = jnp.sum((jnp.cumsum(onehot, axis=0) - onehot) * onehot, axis=1)
    pair_rank = block_rank(bucket_owner, gene_count, owner_count)
    source_start = lax.axis_index("gene") * src_buckets
    mine_owner = lax.dynamic_slice_in_dim(bucket_owner, source_start, src_buckets)
    mine_rank = lax.dynamic_slice_in_dim(pair_rank, source_start, src_buckets)
    own_key = jnp.where(bucket_owner == owner_here, owner_rank, held_slots)
    own_bucket = (
        jnp.zeros((held_slots,), jnp.int32)
        .at[own_key]
        .set(jnp.arange(total_buckets, dtype=jnp.int32), mode="drop")
    )
    own_source = own_bucket // src_buckets
    own_pair = jnp.take(pair_rank, own_bucket)
    cohort_ids = jnp.arange(cohort_count, dtype=jnp.int32)
    flat_index = (
        (own_source[None, :] * cohort_count + cohort_ids[:, None]) * cap_slots + own_pair[None, :]
    ).reshape(cohort_count * held_slots)
    send_from = (
        jnp.full((owner_count * cap_slots,), -1, jnp.int32)
        .at[mine_owner * cap_slots + mine_rank]
        .set(jnp.arange(src_buckets, dtype=jnp.int32))
    )
    send_pick = jnp.maximum(send_from, 0)
    cohort_left = lax.all_gather(left_cols[:, None, :], "cohort", axis=1, tiled=True)
    packed = (
        jnp.take(masked_dosage, send_pick, axis=1)
        * (send_from >= 0).astype(jnp.bfloat16)[None, :, None]
    )
    packed = packed.reshape(sample_rows, owner_count, cap_slots, span_width)
    arrived = lax.all_to_all(packed, ("gene", "cohort"), split_axis=1, concat_axis=1, tiled=True)
    arrived = arrived.reshape(sample_rows, owner_count * cap_slots, span_width)
    owned = jnp.take(arrived, flat_index, axis=1).reshape(
        sample_rows, cohort_count, held_slots, span_width
    )
    gram = jnp.einsum("schj,schk->hjk", owned, owned, preferred_element_type=jnp.float32)
    cross = jnp.einsum("sci,schk->hik", cohort_left, owned, preferred_element_type=jnp.float32)
    slot_start = lax.axis_index("sample") * share
    gram, cross = lax.psum((gram, cross), "sample")
    tiles, squares, burden_sum, trace_sum = finish_slots(
        gram, cross, own_bucket, moments, variant_weight, variant_gene, owner_here, sample_total
    )
    tiles = lax.dynamic_slice_in_dim(tiles, slot_start, share)
    rho_col = jnp.array(RHO_GRID, dtype=jnp.float32)[:, None]
    rho_stats = (
        (1.0 - rho_col) * squares[None, :] + rho_col * (burden_sum * burden_sum)[None, :]
    ) / span_width
    gene_trace = trace_sum / span_width
    return (tiles[None], rho_stats, gene_trace)


UNIT = 200


def contract_rows(first, second):
    return lax.dot_general(
        first, second, (((0,), (0,)), ((), ())), preferred_element_type=jnp.float32
    )


def square_iota():
    shape = (BUCKET_WIDTH, BUCKET_WIDTH)
    return (
        lax.broadcasted_iota(jnp.int32, shape, 0),
        lax.broadcasted_iota(jnp.int32, shape, 1),
    )


def window_kernel(
    covs, sample_total, order_ref, dosage_ref, side_ref, weight_ref, gene_ref,
    tile_ref, rho_ref, trace_ref,
    panel_ref, left_t, own, give, take_core, take_x, take_near, take_far, final, mom_out, mom_in, stats,
    core_send, core_recv, x_send, x_recv, near_send, near_recv, far_send, far_recv,
    swap_send, swap_recv, mom_send, mom_recv, stat_send, stat_recv, panel_sem,
):
    width = BUCKET_WIDTH
    s = lax.axis_index("sample")
    y = lax.axis_index("gene")
    z = lax.axis_index("cohort")
    x, core = s // 2, s % 2
    z_hi, z_lo = z // 2, z % 2
    to_core = {"sample": 2 * x + 1 - core}
    to_x = {"sample": 2 * (1 - x) + core}
    to_corner = {"sample": 2 * (1 - x) + 1 - core}
    to_near = {"cohort": 2 * z_hi + 1 - z_lo}
    to_far = {"cohort": 2 * (1 - z_hi) + z_lo}
    to_swap = {"sample": 2 * y + core, "gene": x}

    def panel_copy(i):
        at = pl.multiple_of(i * width, width)
        return pltpu.make_async_copy(
            dosage_ref.at[:, pl.ds(at, width)], panel_ref.at[i], panel_sem.at[i]
        )

    def fetch(i, carry):
        panel_copy(i).start()
        return carry

    def fetched(i, carry):
        panel_copy(i).wait()
        return carry

    lax.fori_loop(0, panel_ref.shape[0], fetch, 0)

    barrier = pltpu.get_barrier_semaphore()
    for peer in (to_core, to_x, to_corner, to_near, to_far):
        pl.semaphore_signal(barrier, inc=1, device_id=peer)

    @pl.when(x != y)
    def _():
        pl.semaphore_signal(barrier, inc=1, device_id=to_swap)

    pl.semaphore_wait(barrier, 5 + (x + y) % 2)

    def remote(source, target, sent, arrived, peer):
        return pltpu.make_async_remote_copy(
            src_ref=source, dst_ref=target, send_sem=sent, recv_sem=arrived, device_id=peer
        )

    def core_copy(i):
        return remote(give.at[i], take_core.at[i], core_send.at[i], core_recv.at[i], to_core)

    def x_copy(i):
        return remote(own.at[i], take_x.at[i], x_send.at[i], x_recv.at[i], to_x)

    def near_copy(i):
        return remote(own.at[8 + i], take_near.at[i], near_send.at[i], near_recv.at[i], to_near)

    def far_copy(i):
        return remote(own.at[12 + i], take_far.at[i], far_send.at[i], far_recv.at[i], to_far)

    def swap_copy(i):
        return remote(own.at[14 + i], final.at[i], swap_send.at[i], swap_recv.at[i], to_swap)

    def moment_copy(i):
        peer = (to_core, to_x, to_near, to_far)[i]
        return remote(mom_out.at[i], mom_in.at[i], mom_send.at[i], mom_recv.at[i], peer)

    side = side_ref[...]
    keep = jnp.broadcast_to(side[:, covs + 1 : covs + 2], side.shape)
    masked_side = side * keep
    left_t[...] = jnp.transpose(masked_side)[: left_t.shape[0]]
    mom_out[0] = contract_rows(masked_side, masked_side)[:covs]
    moment_copy(0).start()

    row, col = square_iota()

    def products(base):
        panels = []
        for half in range(2):
            panels.append(panel_ref[order_ref[base + half]] * keep)
        first, second = panels
        gram_a = contract_rows(first, first)
        gram_b = contract_rows(second, second)
        left = left_t[...]
        cross_a = jnp.dot(left, first, preferred_element_type=jnp.float32)
        cross_b = jnp.dot(left, second, preferred_element_type=jnp.float32)
        diagonal = jnp.sum(jnp.where(row == col, gram_b, 0.0), axis=0, keepdims=True)
        last = jnp.concatenate(
            [
                cross_a[covs : covs + 1],
                cross_b[covs : covs + 1],
                diagonal,
                jnp.zeros((UNIT - width - 2 * covs - 3, width), jnp.float32),
            ],
            axis=0,
        )
        return jnp.where(row <= col, gram_a, gram_b), cross_a[:covs], cross_b[:covs], last

    def store_unit(ref, i, base):
        packed, cross_a, cross_b, last = products(base)
        ref[i, 0:width] = packed
        ref[i, width : width + covs] = cross_a
        ref[i, width + covs : width + 2 * covs] = cross_b
        ref[i, width + 2 * covs : UNIT] = last

    def table_at(y_to, z_to, core_to, pair):
        return y * 64 + (y_to * 4 + z_to) * 8 + core_to * 4 + pair * 2

    def produce(i, carry):
        @pl.when(i < 16)
        def _():
            keep_side = i // 8
            k = (i % 8) // 2
            pair = i % 2
            y_to = keep_side * x + (1 - keep_side) * (1 - x)
            z_to = 2 * ((z_hi + 1 + k) % 2) + (z_lo + 1 + k // 2) % 2
            store_unit(give, i, table_at(y_to, z_to, 1 - core, pair))
            core_copy(i).start()
            store_unit(own, i, table_at(y_to, z_to, core, pair))

        @pl.when((i >= 1) & (i <= 8))
        def _():
            core_copy(i - 1).wait_recv()
            own[i - 1] = own[i - 1] + take_core[i - 1]
            x_copy(i - 1).start()

        for step in range(3):
            @pl.when(i == 4 * step + 3)
            def _():
                moment_copy(step).wait_recv()
                mom_out[step + 1] = mom_out[step] + mom_in[step]
                moment_copy(step + 1).start()

        return carry

    lax.fori_loop(0, panel_ref.shape[0], fetched, 0)
    lax.fori_loop(0, 16, produce, 0)

    def meet(i):
        core_copy(8 + i).wait_recv()
        x_copy(i).wait_recv()
        return own[8 + i] + take_core[8 + i] + take_x[i]

    def to_neighbour(i, carry):
        own[8 + i] = meet(i)
        near_copy(i).start()
        return carry

    lax.fori_loop(0, 4, to_neighbour, 0)

    moment_copy(3).wait_recv()
    moments = mom_out[3] + mom_in[3]
    r = lax.broadcasted_iota(jnp.int32, (covs, width), 0)
    c = lax.broadcasted_iota(jnp.int32, (covs, width), 1)
    work = jnp.where(c <= covs, moments, jnp.where(c == r + 64, 1.0, 0.0))
    for k in range(covs):
        scale = 1.0 / jnp.sqrt(work[k : k + 1, k : k + 1])
        pivot = work[k : k + 1, :] * scale
        below = work[:, k : k + 1] * scale
        work = jnp.where(r > k, work - below * pivot, jnp.where(r == k, pivot, work))
    half_score = work[:, covs : covs + 1]
    inverse = work[:, 64 : 64 + covs]

    def to_far_side(i, carry):
        part = meet(4 + i)
        near_copy(i).wait_recv()
        own[12 + i] = part + take_near[i]
        far_copy(i).start()
        return carry

    lax.fori_loop(0, 2, to_far_side, 0)

    for i in range(2):
        part = meet(6 + i)
        near_copy(2 + i).wait_recv()
        far_copy(i).wait_recv()
        part = part + take_near[2 + i] + take_far[i]

        @pl.when(x == y)
        def _():
            final[i] = part

        @pl.when(x != y)
        def _():
            own[14 + i] = part
            swap_copy(i).start()

    owner_base = (y * 4 + z) * GENES_OWN
    slot_base = x * 64 + (y * 4 + z) * 8 + core * 4
    squares, sums, traces = [], [], []
    labels = []
    for i in range(2):
        @pl.when(x != y)
        def _():
            swap_copy(i).wait_recv()

        packed = final[i, 0:width]
        mirrored = jnp.transpose(packed)
        last = final[i, width + 2 * covs : UNIT]
        gram_b = jnp.where(row > col, packed, jnp.where(row == col, last[2:3], mirrored))
        grams = (jnp.where(row <= col, packed, mirrored), gram_b)
        for half in range(2):
            cross = final[i, width + half * covs : width + (half + 1) * covs]
            solved = jnp.dot(
                inverse, cross, precision=lax.Precision.HIGHEST,
                preferred_element_type=jnp.float32,
            )
            projected = lax.dot_general(
                solved, solved, (((0,), (0,)), ((), ())), precision=lax.Precision.HIGHEST,
                preferred_element_type=jnp.float32,
            )
            bucket = order_ref[slot_base + 2 * i + half] + x * 64
            label = gene_ref[bucket]
            live = jnp.where(label >= 0, weight_ref[bucket], 0.0)
            across = jnp.broadcast_to(live, (width, width))
            tile = across * jnp.transpose(across) * (grams[half] - projected) / sample_total
            tile_ref[0, 2 * i + half] = tile
            score = last[half : half + 1] - jnp.sum(solved * half_score, axis=0, keepdims=True)
            zscore = live * score / math.sqrt(sample_total)
            squares.append(zscore * zscore)
            sums.append(zscore)
            traces.append(jnp.sum(jnp.where(row == col, tile, 0.0), axis=0, keepdims=True))
            labels.append(label - owner_base)

    gene_row = lax.broadcasted_iota(jnp.int32, (GENES_OWN, width), 0)
    gene_col = lax.broadcasted_iota(jnp.int32, (GENES_OWN, width), 1)
    for n, group in enumerate((squares, sums, traces)):
        total = jnp.zeros((GENES_OWN, width), jnp.float32)
        for label, value in zip(labels, group):
            total = total + jnp.where(label == gene_row, value, 0.0)
        stats[s, n * GENES_OWN : (n + 1) * GENES_OWN] = total

    def stat_copy(n):
        peer = (to_core, to_x, to_corner)[n]
        return remote(stats.at[s], stats.at[s], stat_send.at[n], stat_recv.at[n], peer)

    for n in range(3):
        stat_copy(n).start()
    for n in range(3):
        stat_copy(n).wait_recv()

    def gene_totals(n):
        at = slice(n * GENES_OWN, (n + 1) * GENES_OWN)
        lanes = (stats[0, at] + stats[1, at]) + (stats[2, at] + stats[3, at])
        total = jnp.sum(lanes, axis=1, keepdims=True)
        return jnp.sum(jnp.where(gene_row == gene_col, total, 0.0), axis=0, keepdims=True)

    square, burden, trace = gene_totals(0), gene_totals(1), gene_totals(2)
    rho = jnp.zeros((len(RHO_GRID), width), jnp.float32)
    for n, value in enumerate(RHO_GRID):
        rho = jnp.where(gene_row == n, value, rho)
    rho_all = ((1.0 - rho) * square + rho * (burden * burden)) / width
    rho_ref[...] = rho_all[:, :GENES_OWN]
    trace_ref[...] = trace[:, :GENES_OWN] / width

    def sent_core(i, carry):
        core_copy(i).wait_send()
        return carry

    lax.fori_loop(0, 16, sent_core, 0)

    def sent_x(i, carry):
        x_copy(i).wait_send()
        return carry

    lax.fori_loop(0, 8, sent_x, 0)
    for i in range(4):
        near_copy(i).wait_send()
        moment_copy(i).wait_send()
    for i in range(3):
        stat_copy(i).wait_send()
    for i in range(2):
        far_copy(i).wait_send()

        @pl.when(x != y)
        def _():
            swap_copy(i).wait_send()


def bucket_order(bucket_owner, gene_count, owner_count):
    total = bucket_owner.shape[0]
    bucket = jnp.arange(total, dtype=jnp.int32)
    block = bucket // (total // gene_count)
    label = block * owner_count + bucket_owner
    before = (label[:, None] == label[None, :]) & (bucket[None, :] < bucket[:, None])
    rank = jnp.sum(before.astype(jnp.int32), axis=1)
    place = label * (total // (gene_count * owner_count)) + rank
    inside = bucket % (total // gene_count)
    return jnp.sum(jnp.where(place[None, :] == bucket[:, None], inside[None, :], 0), axis=1)


def shards_fused(
    dosage, covariates, phenotype, sample_mask, variant_weight, bucket_owner, variant_gene
):
    width = BUCKET_WIDTH
    rows, covs = covariates.shape
    total = bucket_owner.shape[0]
    sample_total = rows * lax.axis_size("sample") * lax.axis_size("cohort")
    order = bucket_order(bucket_owner, 2, 8)
    side = jnp.concatenate(
        [
            covariates,
            phenotype[:, None],
            sample_mask.astype(jnp.bfloat16)[:, None],
            jnp.zeros((rows, width - covs - 2), jnp.bfloat16),
        ],
        axis=1,
    )
    vmem = pl.BlockSpec(memory_space=pltpu.VMEM)

    def units(count):
        return pltpu.VMEM((count, UNIT, width), jnp.float32)

    counts = (16, 16, 8, 8, 4, 4, 2, 2, 2, 2, 4, 4, 3, 3)
    counts = counts + (dosage.shape[1] // width,)
    sems = [pltpu.SemaphoreType.DMA((count,)) for count in counts]
    tiles, rho_stats, gene_trace = pl.pallas_call(
        functools.partial(window_kernel, covs, sample_total),
        out_shape=(
            jax.ShapeDtypeStruct((1, 4, width, width), jnp.float32),
            jax.ShapeDtypeStruct((len(RHO_GRID), GENES_OWN), jnp.float32),
            jax.ShapeDtypeStruct((1, GENES_OWN), jnp.float32),
        ),
        in_specs=[pl.BlockSpec(memory_space=pltpu.SMEM), pl.BlockSpec(memory_space=pl.ANY)]
        + [vmem] * 3,
        out_specs=(vmem, vmem, vmem),
        scratch_shapes=[
            pltpu.VMEM((dosage.shape[1] // width, rows, width), jnp.bfloat16),
            pltpu.VMEM((48, rows), jnp.bfloat16),
            units(16), units(16), units(16), units(8), units(4), units(2), units(2),
            pltpu.VMEM((4, covs, width), jnp.float32),
            pltpu.VMEM((4, covs, width), jnp.float32),
            pltpu.VMEM((4, 3 * GENES_OWN, width), jnp.float32),
        ] + sems,
        compiler_params=pltpu.CompilerParams(
            collective_id=0, has_side_effects=True, vmem_limit_bytes=40 * 1024 * 1024
        ),
        cost_estimate=pl.CostEstimate(
            flops=2 * rows * width * 176 * 64, bytes_accessed=2 * dosage.size, transcendentals=0
        ),
    )(
        order, dosage, side,
        variant_weight.reshape(total, 1, width), variant_gene.reshape(total, 1, width),
    )
    return tiles, rho_stats, gene_trace.reshape(GENES_OWN)


def solution(mesh):
    placed = (
        P(("sample", "cohort"), "gene"),
        P(("sample", "cohort"), None),
        P(("sample", "cohort")),
        P(("sample", "cohort")),
        P(),
        P(),
        P(),
    )
    shape = dict(mesh.shape)
    fused = (shape["sample"], shape["gene"], shape["cohort"]) == (4, 2, 4)
    body = shards_fused if fused else shards
    return jax.shard_map(
        body,
        mesh=mesh,
        in_specs=placed,
        out_specs=(
            P(("gene", "cohort"), "sample", None, None),
            P(None, ("gene", "cohort")),
            P(("gene", "cohort")),
        ),
        check_vma=False,
    )
```

```python
import functools
import math

import jax
import jax.numpy as jnp
from jax import lax
from jax.experimental import pallas as pl
from jax.experimental.pallas import tpu as pltpu
from jax.sharding import PartitionSpec as P

BUCKET_WIDTH = 128
GENES_OWN = 8


RHO_GRID = (0.0, 0.01, 0.04, 0.09, 0.16, 0.25, 0.5, 1.0)


def solve_moments(factor, rhs):
    half = lax.linalg.triangular_solve(factor, rhs, left_side=True, lower=True)
    return lax.linalg.triangular_solve(factor, half, left_side=True, lower=True, transpose_a=True)


def inner_rows(first, second):
    return lax.dot_general(
        first, second, (((0,), (0,)), ((), ())), preferred_element_type=jnp.float32
    )


def block_rank(labels, group_count, label_count):
    onehot = (labels[:, None] == jnp.arange(label_count, dtype=jnp.int32)[None, :]).astype(
        jnp.int32
    )
    blocks = onehot.reshape(group_count, labels.shape[0] // group_count, label_count)
    return jnp.sum((jnp.cumsum(blocks, axis=1) - blocks) * blocks, axis=2).reshape(labels.shape[0])


def finish_slots(
    gram, cross, slot_bucket, moments, variant_weight, variant_gene, owner_here, sample_total
):
    cov_count = moments.shape[0]
    slot_count = gram.shape[0]
    span_width = gram.shape[1]
    factor = jnp.linalg.cholesky(moments[:, :cov_count])
    beta_hat = solve_moments(factor, moments[:, cov_count:])[:, 0]
    cov_cross = cross[:, :cov_count, :]
    raw_score = cross[:, cov_count, :]
    stacked = jnp.transpose(cov_cross, (1, 0, 2)).reshape(cov_count, slot_count * span_width)
    solved = solve_moments(factor, stacked).reshape(cov_count, slot_count, span_width)
    projected = jnp.einsum("bcj,cbk->bjk", cov_cross, solved, precision=lax.Precision.HIGHEST)
    scores = raw_score - jnp.einsum(
        "bcj,c->bj", cov_cross, beta_hat, precision=lax.Precision.HIGHEST
    )
    bucket_total = variant_gene.shape[0] // span_width
    weight_rows = jnp.where(variant_gene >= 0, variant_weight, 0.0).reshape(
        bucket_total, span_width
    )
    live_weight = jnp.take(weight_rows, slot_bucket, axis=0)
    tiles = live_weight[:, :, None] * live_weight[:, None, :] * (gram - projected) / sample_total
    zscore = (live_weight * scores / math.sqrt(sample_total)).reshape(slot_count * span_width)
    gene_rows = (
        jnp.take(variant_gene.reshape(bucket_total, span_width), slot_bucket, axis=0)
        - owner_here * GENES_OWN
    )
    member = (
        gene_rows.reshape(slot_count * span_width)[:, None]
        == jnp.arange(GENES_OWN, dtype=jnp.int32)[None, :]
    ).astype(jnp.float32)
    squares = jnp.dot(zscore * zscore, member, precision=lax.Precision.HIGHEST)
    burden_sum = jnp.dot(zscore, member, precision=lax.Precision.HIGHEST)
    diagonal = jnp.diagonal(tiles, axis1=1, axis2=2).reshape(slot_count * span_width)
    trace_sum = jnp.dot(diagonal, member, precision=lax.Precision.HIGHEST)
    return (tiles, squares, burden_sum, trace_sum)


def shards(dosage, covariates, phenotype, sample_mask, variant_weight, bucket_owner, variant_gene):
    gene_count = lax.axis_size("gene")
    cohort_count = lax.axis_size("cohort")
    sample_count = lax.axis_size("sample")
    owner_count = gene_count * cohort_count
    span_width = BUCKET_WIDTH
    sample_rows = dosage.shape[0]
    src_buckets = dosage.shape[1] // span_width
    total_buckets = bucket_owner.shape[0]
    held_slots = total_buckets // owner_count
    cap_slots = held_slots // 2
    share = held_slots // sample_count
    sample_total = sample_rows * sample_count * cohort_count
    cohort_here = lax.axis_index("cohort")
    owner_here = lax.axis_index("gene") * cohort_count + cohort_here
    sample_keep = sample_mask.astype(jnp.bfloat16)
    masked_cov = covariates * sample_keep[:, None]
    left_cols = jnp.concatenate([masked_cov, (phenotype * sample_keep)[:, None]], axis=1)
    moments = lax.psum(
        inner_rows(masked_cov, jnp.concatenate([covariates, phenotype[:, None]], axis=1)),
        ("sample", "cohort"),
    )
    masked_dosage = (dosage * sample_keep[:, None]).reshape(sample_rows, src_buckets, span_width)
    owner_ids = jnp.arange(owner_count, dtype=jnp.int32)
    onehot = (bucket_owner[:, None] == owner_ids[None, :]).astype(jnp.int32)
    owner_rank = jnp.sum((jnp.cumsum(onehot, axis=0) - onehot) * onehot, axis=1)
    pair_rank = block_rank(bucket_owner, gene_count, owner_count)
    source_start = lax.axis_index("gene") * src_buckets
    mine_owner = lax.dynamic_slice_in_dim(bucket_owner, source_start, src_buckets)
    mine_rank = lax.dynamic_slice_in_dim(pair_rank, source_start, src_buckets)
    own_key = jnp.where(bucket_owner == owner_here, owner_rank, held_slots)
    own_bucket = (
        jnp.zeros((held_slots,), jnp.int32)
        .at[own_key]
        .set(jnp.arange(total_buckets, dtype=jnp.int32), mode="drop")
    )
    own_source = own_bucket // src_buckets
    own_pair = jnp.take(pair_rank, own_bucket)
    cohort_ids = jnp.arange(cohort_count, dtype=jnp.int32)
    flat_index = (
        (own_source[None, :] * cohort_count + cohort_ids[:, None]) * cap_slots + own_pair[None, :]
    ).reshape(cohort_count * held_slots)
    send_from = (
        jnp.full((owner_count * cap_slots,), -1, jnp.int32)
        .at[mine_owner * cap_slots + mine_rank]
        .set(jnp.arange(src_buckets, dtype=jnp.int32))
    )
    send_pick = jnp.maximum(send_from, 0)
    cohort_left = lax.all_gather(left_cols[:, None, :], "cohort", axis=1, tiled=True)
    packed = (
        jnp.take(masked_dosage, send_pick, axis=1)
        * (send_from >= 0).astype(jnp.bfloat16)[None, :, None]
    )
    packed = packed.reshape(sample_rows, owner_count, cap_slots, span_width)
    arrived = lax.all_to_all(packed, ("gene", "cohort"), split_axis=1, concat_axis=1, tiled=True)
    arrived = arrived.reshape(sample_rows, owner_count * cap_slots, span_width)
    owned = jnp.take(arrived, flat_index, axis=1).reshape(
        sample_rows, cohort_count, held_slots, span_width
    )
    gram = jnp.einsum("schj,schk->hjk", owned, owned, preferred_element_type=jnp.float32)
    cross = jnp.einsum("sci,schk->hik", cohort_left, owned, preferred_element_type=jnp.float32)
    slot_start = lax.axis_index("sample") * share
    gram, cross = lax.psum((gram, cross), "sample")
    tiles, squares, burden_sum, trace_sum = finish_slots(
        gram, cross, own_bucket, moments, variant_weight, variant_gene, owner_here, sample_total
    )
    tiles = lax.dynamic_slice_in_dim(tiles, slot_start, share)
    rho_col = jnp.array(RHO_GRID, dtype=jnp.float32)[:, None]
    rho_stats = (
        (1.0 - rho_col) * squares[None, :] + rho_col * (burden_sum * burden_sum)[None, :]
    ) / span_width
    gene_trace = trace_sum / span_width
    return (tiles[None], rho_stats, gene_trace)


UNIT = 200


def square_iota():
    shape = (BUCKET_WIDTH, BUCKET_WIDTH)
    return (
        lax.broadcasted_iota(jnp.int32, shape, 0),
        lax.broadcasted_iota(jnp.int32, shape, 1),
    )


def window_kernel(
    covs, sample_total, order_ref, dosage_ref, cov_ref, pheno_ref, mask_ref, weight_hbm, gene_hbm,
    tile_ref, rho_ref, trace_ref,
    weight_ref, gene_ref, panel_ref, left_t, keep_ref, solved_ref, own, give, take_core, take_x, take_near, take_far, final, mom_out, mom_in, stats,
    core_send, core_recv, x_send, x_recv, near_send, near_recv, far_send, far_recv,
    swap_send, swap_recv, mom_send, mom_recv, stat_send, stat_recv, panel_sem,
    table_sem,
):
    width = BUCKET_WIDTH
    s = lax.axis_index("sample")
    y = lax.axis_index("gene")
    z = lax.axis_index("cohort")
    x, core = s // 2, s % 2
    z_hi, z_lo = z // 2, z % 2
    to_core = {"sample": 2 * x + 1 - core}
    to_x = {"sample": 2 * (1 - x) + core}
    to_corner = {"sample": 2 * (1 - x) + 1 - core}
    to_near = {"cohort": 2 * z_hi + 1 - z_lo}
    to_far = {"cohort": 2 * (1 - z_hi) + z_lo}
    to_swap = {"sample": 2 * y + core, "gene": x}

    def panel_copy(i):
        at = pl.multiple_of(i * width, width)
        return pltpu.make_async_copy(
            dosage_ref.at[:, pl.ds(at, width)], panel_ref.at[i], panel_sem.at[i]
        )

    def fetch(i, carry):
        panel_copy(i).start()
        return carry

    def fetched(i, carry):
        panel_copy(i).wait()
        return carry

    lax.fori_loop(0, panel_ref.shape[0], fetch, 0)
    weight_copy = pltpu.make_async_copy(weight_hbm, weight_ref, table_sem.at[0])
    gene_copy = pltpu.make_async_copy(gene_hbm, gene_ref, table_sem.at[1])
    weight_copy.start()
    gene_copy.start()

    barrier = pltpu.get_barrier_semaphore()
    for peer in (to_core, to_x, to_corner, to_near, to_far):
        pl.semaphore_signal(barrier, inc=1, device_id=peer)

    @pl.when(x != y)
    def _():
        pl.semaphore_signal(barrier, inc=1, device_id=to_swap)

    pl.semaphore_wait(barrier, 5 + (x + y) % 2)

    def remote(source, target, sent, arrived, peer):
        return pltpu.make_async_remote_copy(
            src_ref=source, dst_ref=target, send_sem=sent, recv_sem=arrived, device_id=peer
        )

    def core_copy(i):
        return remote(give.at[i], take_core.at[i], core_send.at[i], core_recv.at[i], to_core)

    def x_copy(i):
        return remote(own.at[i], take_x.at[i], x_send.at[i], x_recv.at[i], to_x)

    def near_copy(i):
        return remote(own.at[8 + i], take_near.at[i], near_send.at[i], near_recv.at[i], to_near)

    def far_copy(i):
        return remote(own.at[12 + i], take_far.at[i], far_send.at[i], far_recv.at[i], to_far)

    def swap_copy(i):
        return remote(own.at[14 + i], final.at[i], swap_send.at[i], swap_recv.at[i], to_swap)

    def moment_copy(i):
        peer = (to_core, to_x, to_near, to_far)[i]
        return remote(mom_out.at[i], mom_in.at[i], mom_send.at[i], mom_recv.at[i], peer)

    rows = mask_ref.shape[1]
    keep_ref[...] = jnp.broadcast_to(
        mask_ref[...].astype(jnp.float32), keep_ref.shape
    ).astype(jnp.bfloat16)
    first_row = lax.broadcasted_iota(jnp.int32, (16, rows), 0) == 0
    outcome = jnp.where(first_row, pheno_ref[...].astype(jnp.float32), 0.0).astype(jnp.bfloat16)
    plain = jnp.concatenate([cov_ref[...], outcome], axis=0)
    left_t[...] = plain * keep_ref[: left_t.shape[0]]
    padded = jnp.concatenate(
        [plain, jnp.zeros((width - plain.shape[0], rows), jnp.bfloat16)], axis=0
    )
    mom_out[0] = lax.dot_general(
        left_t[...], padded, (((1,), (1,)), ((), ())), preferred_element_type=jnp.float32
    )[:covs]
    moment_copy(0).start()

    row, col = square_iota()

    def products(base):
        panels = []
        for half in range(2):
            panels.append(panel_ref[order_ref[base + half]])
        left, masks = left_t[...], keep_ref[...]

        def multiply(panel):
            stacked = jnp.concatenate([jnp.transpose(panel) * masks, left], axis=0)
            product = jnp.dot(stacked, panel, preferred_element_type=jnp.float32)
            return product[:width], product[width:]

        gram_a, cross_a = multiply(panels[0])
        gram_b, cross_b = multiply(panels[1])
        diagonal = jnp.sum(jnp.where(row == col, gram_b, 0.0), axis=0, keepdims=True)
        last = jnp.concatenate(
            [
                cross_a[covs : covs + 1],
                cross_b[covs : covs + 1],
                diagonal,
                jnp.zeros((UNIT - width - 2 * covs - 3, width), jnp.float32),
            ],
            axis=0,
        )
        return jnp.where(row <= col, gram_a, gram_b), cross_a[:covs], cross_b[:covs], last

    def store_unit(ref, i, base):
        packed, cross_a, cross_b, last = products(base)
        ref[i, 0:width] = packed
        ref[i, width : width + covs] = cross_a
        ref[i, width + covs : width + 2 * covs] = cross_b
        ref[i, width + 2 * covs : UNIT] = last

    def table_at(y_to, z_to, core_to, pair):
        return y * 64 + (y_to * 4 + z_to) * 8 + core_to * 4 + pair * 2

    def meet(i):
        core_copy(8 + i).wait_recv()
        x_copy(i).wait_recv()
        return own[8 + i] + take_core[8 + i] + take_x[i]

    def produce(i, carry):
        @pl.when(i < 16)
        def _():
            keep_side = i // 8
            k = (i % 8) // 2
            pair = i % 2
            y_to = keep_side * x + (1 - keep_side) * (1 - x)
            z_to = 2 * ((z_hi + 1 + k) % 2) + (z_lo + 1 + k // 2) % 2
            store_unit(give, i, table_at(y_to, z_to, 1 - core, pair))
            core_copy(i).start()
            store_unit(own, i, table_at(y_to, z_to, core, pair))

        @pl.when((i >= 1) & (i <= 8))
        def _():
            core_copy(i - 1).wait_recv()
            own[i - 1] = own[i - 1] + take_core[i - 1]
            x_copy(i - 1).start()

        for step in range(3):
            @pl.when(i == 2 * step + 1)
            def _():
                moment_copy(step).wait_recv()
                mom_out[step + 1] = mom_out[step] + mom_in[step]
                moment_copy(step + 1).start()

        @pl.when((i >= 9) & (i <= 12))
        def _():
            own[i - 1] = meet(i - 9)
            near_copy(i - 9).start()

        @pl.when(i == 8)
        def _():
            moment_copy(3).wait_recv()
            moments = mom_out[3] + mom_in[3]
            r = lax.broadcasted_iota(jnp.int32, (covs, width), 0)
            c = lax.broadcasted_iota(jnp.int32, (covs, width), 1)
            work = jnp.where(c <= covs, moments, jnp.where(c == r + 64, 1.0, 0.0))
            for k in range(covs):
                scale = 1.0 / jnp.sqrt(work[k : k + 1, k : k + 1])
                pivot = work[k : k + 1, :] * scale
                below = work[:, k : k + 1] * scale
                work = jnp.where(r > k, work - below * pivot, jnp.where(r == k, pivot, work))
            solved_ref[...] = work

        return carry

    lax.fori_loop(0, panel_ref.shape[0], fetched, 0)
    lax.fori_loop(0, 16, produce, 0)
    def to_far_side(i, carry):
        part = meet(4 + i)
        near_copy(i).wait_recv()
        own[12 + i] = part + take_near[i]
        far_copy(i).start()
        return carry

    lax.fori_loop(0, 2, to_far_side, 0)

    for i in range(2):
        part = meet(6 + i)
        near_copy(2 + i).wait_recv()
        far_copy(i).wait_recv()
        part = part + take_near[2 + i] + take_far[i]

        @pl.when(x == y)
        def _():
            final[i] = part

        @pl.when(x != y)
        def _():
            own[14 + i] = part
            swap_copy(i).start()

    half_score = solved_ref[:, covs : covs + 1]
    inverse = solved_ref[:, 64 : 64 + covs]
    weight_copy.wait()
    gene_copy.wait()
    owner_base = (y * 4 + z) * GENES_OWN
    slot_base = x * 64 + (y * 4 + z) * 8 + core * 4
    squares, sums, traces = [], [], []
    labels = []
    for i in range(2):
        @pl.when(x != y)
        def _():
            swap_copy(i).wait_recv()

        packed = final[i, 0:width]
        mirrored = jnp.transpose(packed)
        last = final[i, width + 2 * covs : UNIT]
        gram_b = jnp.where(row > col, packed, jnp.where(row == col, last[2:3], mirrored))
        grams = (jnp.where(row <= col, packed, mirrored), gram_b)
        for half in range(2):
            cross = final[i, width + half * covs : width + (half + 1) * covs]
            solved = jnp.dot(
                inverse, cross, precision=lax.Precision.HIGHEST,
                preferred_element_type=jnp.float32,
            )
            projected = lax.dot_general(
                solved, solved, (((0,), (0,)), ((), ())), precision=lax.Precision.HIGHEST,
                preferred_element_type=jnp.float32,
            )
            bucket = order_ref[slot_base + 2 * i + half] + x * 64
            label = gene_ref[bucket]
            live = jnp.where(label >= 0, weight_ref[bucket], 0.0)
            across = jnp.broadcast_to(live, (width, width))
            tile = across * jnp.transpose(across) * (grams[half] - projected) / sample_total
            tile_ref[0, 2 * i + half] = tile
            score = last[half : half + 1] - jnp.sum(solved * half_score, axis=0, keepdims=True)
            zscore = live * score / math.sqrt(sample_total)
            squares.append(zscore * zscore)
            sums.append(zscore)
            traces.append(jnp.sum(jnp.where(row == col, tile, 0.0), axis=0, keepdims=True))
            labels.append(label - owner_base)

    gene_row = lax.broadcasted_iota(jnp.int32, (GENES_OWN, width), 0)
    gene_col = lax.broadcasted_iota(jnp.int32, (GENES_OWN, width), 1)
    for n, group in enumerate((squares, sums, traces)):
        total = jnp.zeros((GENES_OWN, width), jnp.float32)
        for label, value in zip(labels, group):
            total = total + jnp.where(label == gene_row, value, 0.0)
        stats[s, n * GENES_OWN : (n + 1) * GENES_OWN] = total

    def stat_copy(n):
        peer = (to_core, to_x, to_corner)[n]
        return remote(stats.at[s], stats.at[s], stat_send.at[n], stat_recv.at[n], peer)

    for n in range(3):
        stat_copy(n).start()
    for n in range(3):
        stat_copy(n).wait_recv()

    def gene_totals(n):
        at = slice(n * GENES_OWN, (n + 1) * GENES_OWN)
        lanes = (stats[0, at] + stats[1, at]) + (stats[2, at] + stats[3, at])
        total = jnp.sum(lanes, axis=1, keepdims=True)
        return jnp.sum(jnp.where(gene_row == gene_col, total, 0.0), axis=0, keepdims=True)

    square, burden, trace = gene_totals(0), gene_totals(1), gene_totals(2)
    rho = jnp.zeros((len(RHO_GRID), width), jnp.float32)
    for n, value in enumerate(RHO_GRID):
        rho = jnp.where(gene_row == n, value, rho)
    rho_all = ((1.0 - rho) * square + rho * (burden * burden)) / width
    rho_ref[...] = rho_all[:, :GENES_OWN]
    trace_ref[...] = trace[:, :GENES_OWN] / width

    def sent_core(i, carry):
        core_copy(i).wait_send()
        return carry

    lax.fori_loop(0, 16, sent_core, 0)

    def sent_x(i, carry):
        x_copy(i).wait_send()
        return carry

    lax.fori_loop(0, 8, sent_x, 0)
    for i in range(4):
        near_copy(i).wait_send()
        moment_copy(i).wait_send()
    for i in range(3):
        stat_copy(i).wait_send()
    for i in range(2):
        far_copy(i).wait_send()

        @pl.when(x != y)
        def _():
            swap_copy(i).wait_send()


def bucket_order(bucket_owner, gene_count, owner_count):
    total = bucket_owner.shape[0]
    bucket = jnp.arange(total, dtype=jnp.int32)
    block = bucket // (total // gene_count)
    label = block * owner_count + bucket_owner
    before = (label[:, None] == label[None, :]) & (bucket[None, :] < bucket[:, None])
    rank = jnp.sum(before.astype(jnp.int32), axis=1)
    place = label * (total // (gene_count * owner_count)) + rank
    inside = bucket % (total // gene_count)
    return jnp.sum(jnp.where(place[None, :] == bucket[:, None], inside[None, :], 0), axis=1)


def shards_fused(
    dosage, covariates, phenotype, sample_mask, variant_weight, bucket_owner, variant_gene
):
    width = BUCKET_WIDTH
    rows, covs = covariates.shape
    total = bucket_owner.shape[0]
    sample_total = rows * lax.axis_size("sample") * lax.axis_size("cohort")
    order = bucket_order(bucket_owner, 2, 8)
    vmem = pl.BlockSpec(memory_space=pltpu.VMEM)
    hbm = pl.BlockSpec(memory_space=pltpu.HBM)

    def units(count):
        return pltpu.VMEM((count, UNIT, width), jnp.float32)

    counts = (16, 16, 8, 8, 4, 4, 2, 2, 2, 2, 4, 4, 3, 3)
    counts = counts + (dosage.shape[1] // width, 2)
    sems = [pltpu.SemaphoreType.DMA((count,)) for count in counts]
    tiles, rho_stats, gene_trace = pl.pallas_call(
        functools.partial(window_kernel, covs, sample_total),
        out_shape=(
            jax.ShapeDtypeStruct((1, 4, width, width), jnp.float32),
            jax.ShapeDtypeStruct((len(RHO_GRID), GENES_OWN), jnp.float32),
            jax.ShapeDtypeStruct((1, GENES_OWN), jnp.float32),
        ),
        in_specs=[pl.BlockSpec(memory_space=pltpu.SMEM), hbm, vmem, vmem, vmem, hbm, hbm],
        out_specs=(vmem, vmem, vmem),
        scratch_shapes=[
            pltpu.VMEM((total, 1, width), jnp.float32),
            pltpu.VMEM((total, 1, width), jnp.int32),
            pltpu.VMEM((dosage.shape[1] // width, rows, width), jnp.bfloat16),
            pltpu.VMEM((48, rows), jnp.bfloat16),
            pltpu.VMEM((width, rows), jnp.bfloat16),
            pltpu.VMEM((covs, width), jnp.float32),
            units(16), units(16), units(16), units(8), units(4), units(2), units(2),
            pltpu.VMEM((4, covs, width), jnp.float32),
            pltpu.VMEM((4, covs, width), jnp.float32),
            pltpu.VMEM((4, 3 * GENES_OWN, width), jnp.float32),
        ] + sems,
        compiler_params=pltpu.CompilerParams(
            collective_id=0, has_side_effects=True, vmem_limit_bytes=40 * 1024 * 1024
        ),
        cost_estimate=pl.CostEstimate(
            flops=2 * rows * width * 176 * 64, bytes_accessed=2 * dosage.size, transcendentals=0
        ),
    )(
        order, dosage, covariates.T, phenotype.reshape(1, rows), sample_mask.reshape(1, rows),
        variant_weight.reshape(total, 1, width), variant_gene.reshape(total, 1, width),
    )
    return tiles, rho_stats, gene_trace.reshape(GENES_OWN)


def solution(mesh):
    placed = (
        P(("sample", "cohort"), "gene"),
        P(("sample", "cohort"), None),
        P(("sample", "cohort")),
        P(("sample", "cohort")),
        P(),
        P(),
        P(),
    )
    shape = dict(mesh.shape)
    fused = (shape["sample"], shape["gene"], shape["cohort"]) == (4, 2, 4)
    body = shards_fused if fused else shards
    return jax.shard_map(
        body,
        mesh=mesh,
        in_specs=placed,
        out_specs=(
            P(("gene", "cohort"), "sample", None, None),
            P(None, ("gene", "cohort")),
            P(("gene", "cohort")),
        ),
        check_vma=False,
    )
```

```python
import functools
import math

import jax
import jax.numpy as jnp
from jax import lax
from jax.experimental import pallas as pl
from jax.experimental.pallas import tpu as pltpu
from jax.sharding import PartitionSpec as P

BUCKET_WIDTH = 128
GENES_OWN = 8


RHO_GRID = (0.0, 0.01, 0.04, 0.09, 0.16, 0.25, 0.5, 1.0)


def solve_moments(factor, rhs):
    half = lax.linalg.triangular_solve(factor, rhs, left_side=True, lower=True)
    return lax.linalg.triangular_solve(factor, half, left_side=True, lower=True, transpose_a=True)


def inner_rows(first, second):
    return lax.dot_general(
        first, second, (((0,), (0,)), ((), ())), preferred_element_type=jnp.float32
    )


def block_rank(labels, group_count, label_count):
    onehot = (labels[:, None] == jnp.arange(label_count, dtype=jnp.int32)[None, :]).astype(
        jnp.int32
    )
    blocks = onehot.reshape(group_count, labels.shape[0] // group_count, label_count)
    return jnp.sum((jnp.cumsum(blocks, axis=1) - blocks) * blocks, axis=2).reshape(labels.shape[0])


def finish_slots(
    gram, cross, slot_bucket, moments, variant_weight, variant_gene, owner_here, sample_total
):
    cov_count = moments.shape[0]
    slot_count = gram.shape[0]
    span_width = gram.shape[1]
    factor = jnp.linalg.cholesky(moments[:, :cov_count])
    beta_hat = solve_moments(factor, moments[:, cov_count:])[:, 0]
    cov_cross = cross[:, :cov_count, :]
    raw_score = cross[:, cov_count, :]
    stacked = jnp.transpose(cov_cross, (1, 0, 2)).reshape(cov_count, slot_count * span_width)
    solved = solve_moments(factor, stacked).reshape(cov_count, slot_count, span_width)
    projected = jnp.einsum("bcj,cbk->bjk", cov_cross, solved, precision=lax.Precision.HIGHEST)
    scores = raw_score - jnp.einsum(
        "bcj,c->bj", cov_cross, beta_hat, precision=lax.Precision.HIGHEST
    )
    bucket_total = variant_gene.shape[0] // span_width
    weight_rows = jnp.where(variant_gene >= 0, variant_weight, 0.0).reshape(
        bucket_total, span_width
    )
    live_weight = jnp.take(weight_rows, slot_bucket, axis=0)
    tiles = live_weight[:, :, None] * live_weight[:, None, :] * (gram - projected) / sample_total
    zscore = (live_weight * scores / math.sqrt(sample_total)).reshape(slot_count * span_width)
    gene_rows = (
        jnp.take(variant_gene.reshape(bucket_total, span_width), slot_bucket, axis=0)
        - owner_here * GENES_OWN
    )
    member = (
        gene_rows.reshape(slot_count * span_width)[:, None]
        == jnp.arange(GENES_OWN, dtype=jnp.int32)[None, :]
    ).astype(jnp.float32)
    squares = jnp.dot(zscore * zscore, member, precision=lax.Precision.HIGHEST)
    burden_sum = jnp.dot(zscore, member, precision=lax.Precision.HIGHEST)
    diagonal = jnp.diagonal(tiles, axis1=1, axis2=2).reshape(slot_count * span_width)
    trace_sum = jnp.dot(diagonal, member, precision=lax.Precision.HIGHEST)
    return (tiles, squares, burden_sum, trace_sum)


def shards(dosage, covariates, phenotype, sample_mask, variant_weight, bucket_owner, variant_gene):
    gene_count = lax.axis_size("gene")
    cohort_count = lax.axis_size("cohort")
    sample_count = lax.axis_size("sample")
    owner_count = gene_count * cohort_count
    span_width = BUCKET_WIDTH
    sample_rows = dosage.shape[0]
    src_buckets = dosage.shape[1] // span_width
    total_buckets = bucket_owner.shape[0]
    held_slots = total_buckets // owner_count
    cap_slots = held_slots // 2
    share = held_slots // sample_count
    sample_total = sample_rows * sample_count * cohort_count
    cohort_here = lax.axis_index("cohort")
    owner_here = lax.axis_index("gene") * cohort_count + cohort_here
    sample_keep = sample_mask.astype(jnp.bfloat16)
    masked_cov = covariates * sample_keep[:, None]
    left_cols = jnp.concatenate([masked_cov, (phenotype * sample_keep)[:, None]], axis=1)
    moments = lax.psum(
        inner_rows(masked_cov, jnp.concatenate([covariates, phenotype[:, None]], axis=1)),
        ("sample", "cohort"),
    )
    masked_dosage = (dosage * sample_keep[:, None]).reshape(sample_rows, src_buckets, span_width)
    owner_ids = jnp.arange(owner_count, dtype=jnp.int32)
    onehot = (bucket_owner[:, None] == owner_ids[None, :]).astype(jnp.int32)
    owner_rank = jnp.sum((jnp.cumsum(onehot, axis=0) - onehot) * onehot, axis=1)
    pair_rank = block_rank(bucket_owner, gene_count, owner_count)
    source_start = lax.axis_index("gene") * src_buckets
    mine_owner = lax.dynamic_slice_in_dim(bucket_owner, source_start, src_buckets)
    mine_rank = lax.dynamic_slice_in_dim(pair_rank, source_start, src_buckets)
    own_key = jnp.where(bucket_owner == owner_here, owner_rank, held_slots)
    own_bucket = (
        jnp.zeros((held_slots,), jnp.int32)
        .at[own_key]
        .set(jnp.arange(total_buckets, dtype=jnp.int32), mode="drop")
    )
    own_source = own_bucket // src_buckets
    own_pair = jnp.take(pair_rank, own_bucket)
    cohort_ids = jnp.arange(cohort_count, dtype=jnp.int32)
    flat_index = (
        (own_source[None, :] * cohort_count + cohort_ids[:, None]) * cap_slots + own_pair[None, :]
    ).reshape(cohort_count * held_slots)
    send_from = (
        jnp.full((owner_count * cap_slots,), -1, jnp.int32)
        .at[mine_owner * cap_slots + mine_rank]
        .set(jnp.arange(src_buckets, dtype=jnp.int32))
    )
    send_pick = jnp.maximum(send_from, 0)
    cohort_left = lax.all_gather(left_cols[:, None, :], "cohort", axis=1, tiled=True)
    packed = (
        jnp.take(masked_dosage, send_pick, axis=1)
        * (send_from >= 0).astype(jnp.bfloat16)[None, :, None]
    )
    packed = packed.reshape(sample_rows, owner_count, cap_slots, span_width)
    arrived = lax.all_to_all(packed, ("gene", "cohort"), split_axis=1, concat_axis=1, tiled=True)
    arrived = arrived.reshape(sample_rows, owner_count * cap_slots, span_width)
    owned = jnp.take(arrived, flat_index, axis=1).reshape(
        sample_rows, cohort_count, held_slots, span_width
    )
    gram = jnp.einsum("schj,schk->hjk", owned, owned, preferred_element_type=jnp.float32)
    cross = jnp.einsum("sci,schk->hik", cohort_left, owned, preferred_element_type=jnp.float32)
    slot_start = lax.axis_index("sample") * share
    gram, cross = lax.psum((gram, cross), "sample")
    tiles, squares, burden_sum, trace_sum = finish_slots(
        gram, cross, own_bucket, moments, variant_weight, variant_gene, owner_here, sample_total
    )
    tiles = lax.dynamic_slice_in_dim(tiles, slot_start, share)
    rho_col = jnp.array(RHO_GRID, dtype=jnp.float32)[:, None]
    rho_stats = (
        (1.0 - rho_col) * squares[None, :] + rho_col * (burden_sum * burden_sum)[None, :]
    ) / span_width
    gene_trace = trace_sum / span_width
    return (tiles[None], rho_stats, gene_trace)


UNIT = 200


def square_iota():
    shape = (BUCKET_WIDTH, BUCKET_WIDTH)
    return (
        lax.broadcasted_iota(jnp.int32, shape, 0),
        lax.broadcasted_iota(jnp.int32, shape, 1),
    )


def window_kernel(
    covs, sample_total, order_ref, dosage_ref, cov_ref, pheno_ref, mask_ref, weight_hbm, gene_hbm,
    tile_ref, rho_ref, trace_ref,
    weight_ref, gene_ref, panel_ref, left_t, keep_ref, solved_ref, own, give, take_core, take_x, take_near, take_far, final, mom_out, mom_in, stats,
    core_send, core_recv, x_send, x_recv, near_send, near_recv, far_send, far_recv,
    swap_send, swap_recv, mom_send, mom_recv, stat_send, stat_recv, panel_sem,
    table_sem,
):
    width = BUCKET_WIDTH
    s = lax.axis_index("sample")
    y = lax.axis_index("gene")
    z = lax.axis_index("cohort")
    x, core = s // 2, s % 2
    z_hi, z_lo = z // 2, z % 2
    to_core = {"sample": 2 * x + 1 - core}
    to_x = {"sample": 2 * (1 - x) + core}
    to_corner = {"sample": 2 * (1 - x) + 1 - core}
    to_near = {"cohort": 2 * z_hi + 1 - z_lo}
    to_far = {"cohort": 2 * (1 - z_hi) + z_lo}
    to_swap = {"sample": 2 * y + core, "gene": x}

    def panel_copy(i):
        at = pl.multiple_of(i * width, width)
        return pltpu.make_async_copy(
            dosage_ref.at[:, pl.ds(at, width)], panel_ref.at[i], panel_sem.at[i]
        )

    def fetch(i, carry):
        panel_copy(i).start()
        return carry

    def fetched(i, carry):
        panel_copy(i).wait()
        return carry

    lax.fori_loop(0, panel_ref.shape[0], fetch, 0)
    weight_copy = pltpu.make_async_copy(weight_hbm, weight_ref, table_sem.at[0])
    gene_copy = pltpu.make_async_copy(gene_hbm, gene_ref, table_sem.at[1])
    weight_copy.start()
    gene_copy.start()

    barrier = pltpu.get_barrier_semaphore()
    for peer in (to_core, to_x, to_corner, to_near, to_far):
        pl.semaphore_signal(barrier, inc=1, device_id=peer)

    @pl.when(x != y)
    def _():
        pl.semaphore_signal(barrier, inc=1, device_id=to_swap)

    pl.semaphore_wait(barrier, 5 + (x + y) % 2)

    def remote(source, target, sent, arrived, peer):
        return pltpu.make_async_remote_copy(
            src_ref=source, dst_ref=target, send_sem=sent, recv_sem=arrived, device_id=peer
        )

    def core_copy(i):
        return remote(give.at[i], take_core.at[i], core_send.at[i], core_recv.at[i], to_core)

    def x_copy(i):
        return remote(own.at[i], take_x.at[i], x_send.at[i], x_recv.at[i], to_x)

    def near_copy(i):
        return remote(own.at[8 + i], take_near.at[i], near_send.at[i], near_recv.at[i], to_near)

    def far_copy(i):
        return remote(own.at[12 + i], take_far.at[i], far_send.at[i], far_recv.at[i], to_far)

    def swap_copy(i):
        return remote(own.at[14 + i], final.at[i], swap_send.at[i], swap_recv.at[i], to_swap)

    def moment_copy(i):
        peer = (to_core, to_x, to_near, to_far)[i]
        return remote(mom_out.at[i], mom_in.at[i], mom_send.at[i], mom_recv.at[i], peer)

    rows = mask_ref.shape[1]
    keep_ref[...] = jnp.broadcast_to(
        mask_ref[...].astype(jnp.float32), keep_ref.shape
    ).astype(jnp.bfloat16)
    first_row = lax.broadcasted_iota(jnp.int32, (16, rows), 0) == 0
    outcome = jnp.where(first_row, pheno_ref[...].astype(jnp.float32), 0.0).astype(jnp.bfloat16)
    plain = jnp.concatenate([cov_ref[...], outcome], axis=0)
    left_t[...] = plain * keep_ref[: left_t.shape[0]]
    padded = jnp.concatenate(
        [plain, jnp.zeros((width - plain.shape[0], rows), jnp.bfloat16)], axis=0
    )
    mom_out[0] = lax.dot_general(
        left_t[...], padded, (((1,), (1,)), ((), ())), preferred_element_type=jnp.float32
    )[:covs]
    moment_copy(0).start()

    row, col = square_iota()

    def products(base):
        panels = []
        for half in range(2):
            panels.append(panel_ref[order_ref[base + half]])
        left, masks = left_t[...], keep_ref[...]

        def multiply(panel):
            stacked = jnp.concatenate([jnp.transpose(panel) * masks, left], axis=0)
            product = jnp.dot(stacked, panel, preferred_element_type=jnp.float32)
            return product[:width], product[width:]

        gram_a, cross_a = multiply(panels[0])
        gram_b, cross_b = multiply(panels[1])
        diagonal = jnp.sum(jnp.where(row == col, gram_b, 0.0), axis=0, keepdims=True)
        last = jnp.concatenate(
            [
                cross_a[covs : covs + 1],
                cross_b[covs : covs + 1],
                diagonal,
                jnp.zeros((UNIT - width - 2 * covs - 3, width), jnp.float32),
            ],
            axis=0,
        )
        return jnp.where(row <= col, gram_a, gram_b), cross_a[:covs], cross_b[:covs], last

    def store_unit(ref, i, base):
        packed, cross_a, cross_b, last = products(base)
        ref[i, 0:width] = packed
        ref[i, width : width + covs] = cross_a
        ref[i, width + covs : width + 2 * covs] = cross_b
        ref[i, width + 2 * covs : UNIT] = last

    def table_at(y_to, z_to, core_to, pair):
        return y * 64 + (y_to * 4 + z_to) * 8 + core_to * 4 + pair * 2

    def meet(i):
        core_copy(8 + i).wait_recv()
        x_copy(i).wait_recv()
        return own[8 + i] + take_core[8 + i] + take_x[i]

    def produce(i, carry):
        @pl.when(i < 16)
        def _():
            keep_side = i // 8
            k = (i % 8) // 2
            pair = i % 2
            y_to = keep_side * x + (1 - keep_side) * (1 - x)
            z_to = 2 * ((z_hi + 1 + k) % 2) + (z_lo + 1 + k // 2) % 2
            store_unit(give, i, table_at(y_to, z_to, 1 - core, pair))
            core_copy(i).start()
            store_unit(own, i, table_at(y_to, z_to, core, pair))

        @pl.when((i >= 1) & (i <= 8))
        def _():
            core_copy(i - 1).wait_recv()
            own[i - 1] = own[i - 1] + take_core[i - 1]
            x_copy(i - 1).start()

        for step in range(3):
            @pl.when(i == 2 * step + 1)
            def _():
                moment_copy(step).wait_recv()
                mom_out[step + 1] = mom_out[step] + mom_in[step]
                moment_copy(step + 1).start()

        @pl.when((i >= 9) & (i <= 12))
        def _():
            own[i - 1] = meet(i - 9)
            near_copy(i - 9).start()

        @pl.when(i == 8)
        def _():
            moment_copy(3).wait_recv()
            moments = mom_out[3] + mom_in[3]
            r = lax.broadcasted_iota(jnp.int32, (covs, width), 0)
            c = lax.broadcasted_iota(jnp.int32, (covs, width), 1)
            work = jnp.where(c <= covs, moments, jnp.where(c == r + 64, 1.0, 0.0))
            for k in range(covs):
                scale = 1.0 / jnp.sqrt(work[k : k + 1, k : k + 1])
                pivot = work[k : k + 1, :] * scale
                below = work[:, k : k + 1] * scale
                work = jnp.where(r > k, work - below * pivot, jnp.where(r == k, pivot, work))
            solved_ref[...] = work

        return carry

    lax.fori_loop(0, panel_ref.shape[0], fetched, 0)
    lax.fori_loop(0, 16, produce, 0)
    def to_far_side(i, carry):
        part = meet(4 + i)
        near_copy(i).wait_recv()
        own[12 + i] = part + take_near[i]
        far_copy(i).start()
        return carry

    lax.fori_loop(0, 2, to_far_side, 0)

    for i in range(2):
        part = meet(6 + i)
        near_copy(2 + i).wait_recv()
        far_copy(i).wait_recv()
        part = part + take_near[2 + i] + take_far[i]

        @pl.when(x == y)
        def _():
            final[i] = part

        @pl.when(x != y)
        def _():
            own[14 + i] = part
            swap_copy(i).start()

    half_score = solved_ref[:, covs : covs + 1]
    inverse = solved_ref[:, 64 : 64 + covs]
    weight_copy.wait()
    gene_copy.wait()
    owner_base = (y * 4 + z) * GENES_OWN
    slot_base = x * 64 + (y * 4 + z) * 8 + core * 4
    squares, sums, traces = [], [], []
    labels = []
    for i in range(2):
        @pl.when(x != y)
        def _():
            swap_copy(i).wait_recv()

        packed = final[i, 0:width]
        mirrored = jnp.transpose(packed)
        last = final[i, width + 2 * covs : UNIT]
        gram_b = jnp.where(row > col, packed, jnp.where(row == col, last[2:3], mirrored))
        grams = (jnp.where(row <= col, packed, mirrored), gram_b)
        for half in range(2):
            cross = final[i, width + half * covs : width + (half + 1) * covs]
            solved = jnp.dot(
                inverse, cross, precision=lax.Precision.HIGHEST,
                preferred_element_type=jnp.float32,
            )
            projected = lax.dot_general(
                solved, solved, (((0,), (0,)), ((), ())), precision=lax.Precision.HIGHEST,
                preferred_element_type=jnp.float32,
            )
            bucket = order_ref[slot_base + 2 * i + half] + x * 64
            label = gene_ref[bucket]
            live = jnp.where(label >= 0, weight_ref[bucket], 0.0)
            across = jnp.broadcast_to(live, (width, width))
            tile = across * jnp.transpose(across) * (grams[half] - projected) / sample_total
            tile_ref[0, 2 * i + half] = tile
            score = last[half : half + 1] - jnp.sum(solved * half_score, axis=0, keepdims=True)
            zscore = live * score / math.sqrt(sample_total)
            squares.append(zscore * zscore)
            sums.append(zscore)
            traces.append(jnp.sum(jnp.where(row == col, tile, 0.0), axis=0, keepdims=True))
            labels.append(label - owner_base)

    gene_row = lax.broadcasted_iota(jnp.int32, (GENES_OWN, width), 0)
    gene_col = lax.broadcasted_iota(jnp.int32, (GENES_OWN, width), 1)
    for n, group in enumerate((squares, sums, traces)):
        total = jnp.zeros((GENES_OWN, width), jnp.float32)
        for label, value in zip(labels, group):
            total = total + jnp.where(label == gene_row, value, 0.0)
        stats[s, n * GENES_OWN : (n + 1) * GENES_OWN] = total

    def stat_copy(n):
        peer = (to_core, to_x, to_corner)[n]
        return remote(stats.at[s], stats.at[s], stat_send.at[n], stat_recv.at[n], peer)

    for n in range(3):
        stat_copy(n).start()
    for n in range(3):
        stat_copy(n).wait_recv()

    def gene_totals(n):
        at = slice(n * GENES_OWN, (n + 1) * GENES_OWN)
        lanes = (stats[0, at] + stats[1, at]) + (stats[2, at] + stats[3, at])
        total = jnp.sum(lanes, axis=1, keepdims=True)
        return jnp.sum(jnp.where(gene_row == gene_col, total, 0.0), axis=0, keepdims=True)

    square, burden, trace = gene_totals(0), gene_totals(1), gene_totals(2)
    rho = jnp.zeros((len(RHO_GRID), width), jnp.float32)
    for n, value in enumerate(RHO_GRID):
        rho = jnp.where(gene_row == n, value, rho)
    rho_all = ((1.0 - rho) * square + rho * (burden * burden)) / width
    rho_ref[...] = rho_all[:, :GENES_OWN]
    trace_ref[...] = trace[:, :GENES_OWN] / width

    def sent_core(i, carry):
        core_copy(i).wait_send()
        return carry

    lax.fori_loop(0, 16, sent_core, 0)

    def sent_x(i, carry):
        x_copy(i).wait_send()
        return carry

    lax.fori_loop(0, 8, sent_x, 0)
    for i in range(4):
        near_copy(i).wait_send()
        moment_copy(i).wait_send()
    for i in range(3):
        stat_copy(i).wait_send()
    for i in range(2):
        far_copy(i).wait_send()

        @pl.when(x != y)
        def _():
            swap_copy(i).wait_send()


def bucket_order(bucket_owner, gene_count, owner_count):
    total = bucket_owner.shape[0]
    bucket = jnp.arange(total, dtype=jnp.int32)
    block = bucket // (total // gene_count)
    label = block * owner_count + bucket_owner
    before = (label[:, None] == label[None, :]) & (bucket[None, :] < bucket[:, None])
    rank = jnp.sum(before.astype(jnp.int32), axis=1)
    place = label * (total // (gene_count * owner_count)) + rank
    inside = bucket % (total // gene_count)
    return jnp.sum(jnp.where(place[None, :] == bucket[:, None], inside[None, :], 0), axis=1)


def shards_fused(
    dosage, covariates, phenotype, sample_mask, variant_weight, bucket_owner, variant_gene
):
    width = BUCKET_WIDTH
    rows, covs = covariates.shape
    total = bucket_owner.shape[0]
    sample_total = rows * lax.axis_size("sample") * lax.axis_size("cohort")
    order = bucket_order(bucket_owner, 2, 8)
    vmem = pl.BlockSpec(memory_space=pltpu.VMEM)
    hbm = pl.BlockSpec(memory_space=pltpu.HBM)

    def units(count):
        return pltpu.VMEM((count, UNIT, width), jnp.float32)

    counts = (16, 16, 8, 8, 4, 4, 2, 2, 2, 2, 4, 4, 3, 3)
    counts = counts + (dosage.shape[1] // width, 2)
    sems = [pltpu.SemaphoreType.DMA((count,)) for count in counts]
    tiles, rho_stats, gene_trace = pl.pallas_call(
        functools.partial(window_kernel, covs, sample_total),
        out_shape=(
            jax.ShapeDtypeStruct((1, 4, width, width), jnp.float32),
            jax.ShapeDtypeStruct((len(RHO_GRID), GENES_OWN), jnp.float32),
            jax.ShapeDtypeStruct((1, GENES_OWN), jnp.float32),
        ),
        in_specs=[pl.BlockSpec(memory_space=pltpu.SMEM), hbm, vmem, vmem, vmem, hbm, hbm],
        out_specs=(vmem, vmem, vmem),
        scratch_shapes=[
            pltpu.VMEM((total, 1, width), jnp.float32),
            pltpu.VMEM((total, 1, width), jnp.int32),
            pltpu.VMEM((dosage.shape[1] // width, rows, width), jnp.bfloat16),
            pltpu.VMEM((48, rows), jnp.bfloat16),
            pltpu.VMEM((width, rows), jnp.bfloat16),
            pltpu.VMEM((covs, width), jnp.float32),
            units(16), units(16), units(16), units(8), units(4), units(2), units(2),
            pltpu.VMEM((4, covs, width), jnp.float32),
            pltpu.VMEM((4, covs, width), jnp.float32),
            pltpu.VMEM((4, 3 * GENES_OWN, width), jnp.float32),
        ] + sems,
        compiler_params=pltpu.CompilerParams(
            collective_id=0, has_side_effects=True, vmem_limit_bytes=62 * 1024 * 1024
        ),
        cost_estimate=pl.CostEstimate(
            flops=2 * rows * width * 176 * 64, bytes_accessed=2 * dosage.size, transcendentals=0
        ),
    )(
        order, dosage, covariates.T, phenotype.reshape(1, rows), sample_mask.reshape(1, rows),
        variant_weight.reshape(total, 1, width), variant_gene.reshape(total, 1, width),
    )
    return tiles, rho_stats, gene_trace.reshape(GENES_OWN)


def solution(mesh):
    placed = (
        P(("sample", "cohort"), "gene"),
        P(("sample", "cohort"), None),
        P(("sample", "cohort")),
        P(("sample", "cohort")),
        P(),
        P(),
        P(),
    )
    shape = dict(mesh.shape)
    fused = (shape["sample"], shape["gene"], shape["cohort"]) == (4, 2, 4)
    body = shards_fused if fused else shards
    return jax.shard_map(
        body,
        mesh=mesh,
        in_specs=placed,
        out_specs=(
            P(("gene", "cohort"), "sample", None, None),
            P(None, ("gene", "cohort")),
            P(("gene", "cohort")),
        ),
        check_vma=False,
    )
```

```python
import functools
import math

import jax
import jax.numpy as jnp
from jax import lax
from jax.experimental import pallas as pl
from jax.experimental.pallas import tpu as pltpu
from jax.sharding import PartitionSpec as P

BUCKET_WIDTH = 128
GENES_OWN = 8


RHO_GRID = (0.0, 0.01, 0.04, 0.09, 0.16, 0.25, 0.5, 1.0)


def solve_moments(factor, rhs):
    half = lax.linalg.triangular_solve(factor, rhs, left_side=True, lower=True)
    return lax.linalg.triangular_solve(factor, half, left_side=True, lower=True, transpose_a=True)


def inner_rows(first, second):
    return lax.dot_general(
        first, second, (((0,), (0,)), ((), ())), preferred_element_type=jnp.float32
    )


def block_rank(labels, group_count, label_count):
    onehot = (labels[:, None] == jnp.arange(label_count, dtype=jnp.int32)[None, :]).astype(
        jnp.int32
    )
    blocks = onehot.reshape(group_count, labels.shape[0] // group_count, label_count)
    return jnp.sum((jnp.cumsum(blocks, axis=1) - blocks) * blocks, axis=2).reshape(labels.shape[0])


def finish_slots(
    gram, cross, slot_bucket, moments, variant_weight, variant_gene, owner_here, sample_total
):
    cov_count = moments.shape[0]
    slot_count = gram.shape[0]
    span_width = gram.shape[1]
    factor = jnp.linalg.cholesky(moments[:, :cov_count])
    beta_hat = solve_moments(factor, moments[:, cov_count:])[:, 0]
    cov_cross = cross[:, :cov_count, :]
    raw_score = cross[:, cov_count, :]
    stacked = jnp.transpose(cov_cross, (1, 0, 2)).reshape(cov_count, slot_count * span_width)
    solved = solve_moments(factor, stacked).reshape(cov_count, slot_count, span_width)
    projected = jnp.einsum("bcj,cbk->bjk", cov_cross, solved, precision=lax.Precision.HIGHEST)
    scores = raw_score - jnp.einsum(
        "bcj,c->bj", cov_cross, beta_hat, precision=lax.Precision.HIGHEST
    )
    bucket_total = variant_gene.shape[0] // span_width
    weight_rows = jnp.where(variant_gene >= 0, variant_weight, 0.0).reshape(
        bucket_total, span_width
    )
    live_weight = jnp.take(weight_rows, slot_bucket, axis=0)
    tiles = live_weight[:, :, None] * live_weight[:, None, :] * (gram - projected) / sample_total
    zscore = (live_weight * scores / math.sqrt(sample_total)).reshape(slot_count * span_width)
    gene_rows = (
        jnp.take(variant_gene.reshape(bucket_total, span_width), slot_bucket, axis=0)
        - owner_here * GENES_OWN
    )
    member = (
        gene_rows.reshape(slot_count * span_width)[:, None]
        == jnp.arange(GENES_OWN, dtype=jnp.int32)[None, :]
    ).astype(jnp.float32)
    squares = jnp.dot(zscore * zscore, member, precision=lax.Precision.HIGHEST)
    burden_sum = jnp.dot(zscore, member, precision=lax.Precision.HIGHEST)
    diagonal = jnp.diagonal(tiles, axis1=1, axis2=2).reshape(slot_count * span_width)
    trace_sum = jnp.dot(diagonal, member, precision=lax.Precision.HIGHEST)
    return (tiles, squares, burden_sum, trace_sum)


def shards(dosage, covariates, phenotype, sample_mask, variant_weight, bucket_owner, variant_gene):
    gene_count = lax.axis_size("gene")
    cohort_count = lax.axis_size("cohort")
    sample_count = lax.axis_size("sample")
    owner_count = gene_count * cohort_count
    span_width = BUCKET_WIDTH
    sample_rows = dosage.shape[0]
    src_buckets = dosage.shape[1] // span_width
    total_buckets = bucket_owner.shape[0]
    held_slots = total_buckets // owner_count
    cap_slots = held_slots // 2
    share = held_slots // sample_count
    sample_total = sample_rows * sample_count * cohort_count
    cohort_here = lax.axis_index("cohort")
    owner_here = lax.axis_index("gene") * cohort_count + cohort_here
    sample_keep = sample_mask.astype(jnp.bfloat16)
    masked_cov = covariates * sample_keep[:, None]
    left_cols = jnp.concatenate([masked_cov, (phenotype * sample_keep)[:, None]], axis=1)
    moments = lax.psum(
        inner_rows(masked_cov, jnp.concatenate([covariates, phenotype[:, None]], axis=1)),
        ("sample", "cohort"),
    )
    masked_dosage = (dosage * sample_keep[:, None]).reshape(sample_rows, src_buckets, span_width)
    owner_ids = jnp.arange(owner_count, dtype=jnp.int32)
    onehot = (bucket_owner[:, None] == owner_ids[None, :]).astype(jnp.int32)
    owner_rank = jnp.sum((jnp.cumsum(onehot, axis=0) - onehot) * onehot, axis=1)
    pair_rank = block_rank(bucket_owner, gene_count, owner_count)
    source_start = lax.axis_index("gene") * src_buckets
    mine_owner = lax.dynamic_slice_in_dim(bucket_owner, source_start, src_buckets)
    mine_rank = lax.dynamic_slice_in_dim(pair_rank, source_start, src_buckets)
    own_key = jnp.where(bucket_owner == owner_here, owner_rank, held_slots)
    own_bucket = (
        jnp.zeros((held_slots,), jnp.int32)
        .at[own_key]
        .set(jnp.arange(total_buckets, dtype=jnp.int32), mode="drop")
    )
    own_source = own_bucket // src_buckets
    own_pair = jnp.take(pair_rank, own_bucket)
    cohort_ids = jnp.arange(cohort_count, dtype=jnp.int32)
    flat_index = (
        (own_source[None, :] * cohort_count + cohort_ids[:, None]) * cap_slots + own_pair[None, :]
    ).reshape(cohort_count * held_slots)
    send_from = (
        jnp.full((owner_count * cap_slots,), -1, jnp.int32)
        .at[mine_owner * cap_slots + mine_rank]
        .set(jnp.arange(src_buckets, dtype=jnp.int32))
    )
    send_pick = jnp.maximum(send_from, 0)
    cohort_left = lax.all_gather(left_cols[:, None, :], "cohort", axis=1, tiled=True)
    packed = (
        jnp.take(masked_dosage, send_pick, axis=1)
        * (send_from >= 0).astype(jnp.bfloat16)[None, :, None]
    )
    packed = packed.reshape(sample_rows, owner_count, cap_slots, span_width)
    arrived = lax.all_to_all(packed, ("gene", "cohort"), split_axis=1, concat_axis=1, tiled=True)
    arrived = arrived.reshape(sample_rows, owner_count * cap_slots, span_width)
    owned = jnp.take(arrived, flat_index, axis=1).reshape(
        sample_rows, cohort_count, held_slots, span_width
    )
    gram = jnp.einsum("schj,schk->hjk", owned, owned, preferred_element_type=jnp.float32)
    cross = jnp.einsum("sci,schk->hik", cohort_left, owned, preferred_element_type=jnp.float32)
    slot_start = lax.axis_index("sample") * share
    gram, cross = lax.psum((gram, cross), "sample")
    tiles, squares, burden_sum, trace_sum = finish_slots(
        gram, cross, own_bucket, moments, variant_weight, variant_gene, owner_here, sample_total
    )
    tiles = lax.dynamic_slice_in_dim(tiles, slot_start, share)
    rho_col = jnp.array(RHO_GRID, dtype=jnp.float32)[:, None]
    rho_stats = (
        (1.0 - rho_col) * squares[None, :] + rho_col * (burden_sum * burden_sum)[None, :]
    ) / span_width
    gene_trace = trace_sum / span_width
    return (tiles[None], rho_stats, gene_trace)


UNIT = 200


def square_iota():
    shape = (BUCKET_WIDTH, BUCKET_WIDTH)
    return (
        lax.broadcasted_iota(jnp.int32, shape, 0),
        lax.broadcasted_iota(jnp.int32, shape, 1),
    )


def window_kernel(
    covs, sample_total, order_ref, dosage_ref, cov_ref, pheno_ref, mask_ref, weight_hbm, gene_hbm,
    tile_ref, rho_ref, trace_ref,
    weight_ref, gene_ref, panel_ref, left_t, keep_ref, solved_ref, own, give, take_core, take_x, take_near, take_far, final, mom_out, mom_in, stats,
    core_send, core_recv, x_send, x_recv, near_send, near_recv, far_send, far_recv,
    swap_send, swap_recv, mom_send, mom_recv, stat_send, stat_recv, panel_sem,
    table_sem,
):
    width = BUCKET_WIDTH
    s = lax.axis_index("sample")
    y = lax.axis_index("gene")
    z = lax.axis_index("cohort")
    x, core = s // 2, s % 2
    z_hi, z_lo = z // 2, z % 2
    to_core = {"sample": 2 * x + 1 - core}
    to_x = {"sample": 2 * (1 - x) + core}
    to_corner = {"sample": 2 * (1 - x) + 1 - core}
    to_near = {"cohort": 2 * z_hi + 1 - z_lo}
    to_far = {"cohort": 2 * (1 - z_hi) + z_lo}
    to_swap = {"sample": 2 * y + core, "gene": x}

    def panel_copy(i):
        at = pl.multiple_of(i * width, width)
        return pltpu.make_async_copy(
            dosage_ref.at[:, pl.ds(at, width)], panel_ref.at[i], panel_sem.at[i]
        )

    def fetch(i, carry):
        panel_copy(i).start()
        return carry

    def fetched(i, carry):
        panel_copy(i).wait()
        return carry

    lax.fori_loop(0, panel_ref.shape[0], fetch, 0)
    weight_copy = pltpu.make_async_copy(weight_hbm, weight_ref, table_sem.at[0])
    gene_copy = pltpu.make_async_copy(gene_hbm, gene_ref, table_sem.at[1])
    weight_copy.start()
    gene_copy.start()

    barrier = pltpu.get_barrier_semaphore()
    for peer in (to_core, to_x, to_corner, to_near, to_far):
        pl.semaphore_signal(barrier, inc=1, device_id=peer)

    @pl.when(x != y)
    def _():
        pl.semaphore_signal(barrier, inc=1, device_id=to_swap)

    pl.semaphore_wait(barrier, 5 + (x + y) % 2)

    def remote(source, target, sent, arrived, peer):
        return pltpu.make_async_remote_copy(
            src_ref=source, dst_ref=target, send_sem=sent, recv_sem=arrived, device_id=peer
        )

    def core_copy(i):
        return remote(give.at[i], take_core.at[i], core_send.at[i], core_recv.at[i], to_core)

    def x_copy(i):
        return remote(own.at[i], take_x.at[i], x_send.at[i], x_recv.at[i], to_x)

    def near_copy(i):
        return remote(own.at[8 + i], take_near.at[i], near_send.at[i], near_recv.at[i], to_near)

    def far_copy(i):
        return remote(own.at[12 + i], take_far.at[i], far_send.at[i], far_recv.at[i], to_far)

    def swap_copy(i):
        return remote(own.at[14 + i], final.at[i], swap_send.at[i], swap_recv.at[i], to_swap)

    def moment_copy(i):
        peer = (to_core, to_x, to_near, to_far)[i]
        return remote(mom_out.at[i], mom_in.at[i], mom_send.at[i], mom_recv.at[i], peer)

    rows = mask_ref.shape[1]
    keep_ref[...] = jnp.broadcast_to(
        mask_ref[...].astype(jnp.float32), keep_ref.shape
    ).astype(jnp.bfloat16)
    first_row = lax.broadcasted_iota(jnp.int32, (16, rows), 0) == 0
    outcome = jnp.where(first_row, pheno_ref[...].astype(jnp.float32), 0.0).astype(jnp.bfloat16)
    plain = jnp.concatenate([cov_ref[...], outcome], axis=0)
    left_t[...] = plain * keep_ref[: left_t.shape[0]]
    padded = jnp.concatenate(
        [plain, jnp.zeros((width - plain.shape[0], rows), jnp.bfloat16)], axis=0
    )
    mom_out[0] = lax.dot_general(
        left_t[...], padded, (((1,), (1,)), ((), ())), preferred_element_type=jnp.float32
    )[:covs]
    moment_copy(0).start()

    row, col = square_iota()

    def products(base):
        panels = []
        for half in range(2):
            panels.append(panel_ref[order_ref[base + half]])
        left, masks = left_t[...], keep_ref[...]

        def multiply(panel):
            stacked = jnp.concatenate([jnp.transpose(panel) * masks, left], axis=0)
            product = jnp.dot(stacked, panel, preferred_element_type=jnp.float32)
            return product[:width], product[width:]

        gram_a, cross_a = multiply(panels[0])
        gram_b, cross_b = multiply(panels[1])
        diagonal = jnp.sum(jnp.where(row == col, gram_b, 0.0), axis=0, keepdims=True)
        last = jnp.concatenate(
            [
                cross_a[covs : covs + 1],
                cross_b[covs : covs + 1],
                diagonal,
                jnp.zeros((UNIT - width - 2 * covs - 3, width), jnp.float32),
            ],
            axis=0,
        )
        return jnp.where(row <= col, gram_a, gram_b), cross_a[:covs], cross_b[:covs], last

    def store_unit(ref, i, base):
        packed, cross_a, cross_b, last = products(base)
        ref[i, 0:width] = packed
        ref[i, width : width + covs] = cross_a
        ref[i, width + covs : width + 2 * covs] = cross_b
        ref[i, width + 2 * covs : UNIT] = last

    def table_at(y_to, z_to, core_to, pair):
        return y * 64 + (y_to * 4 + z_to) * 8 + core_to * 4 + pair * 2

    def meet(i):
        core_copy(8 + i).wait_recv()
        x_copy(i).wait_recv()
        return own[8 + i] + take_core[8 + i] + take_x[i]

    def close(i):
        part = meet(6 + i)
        near_copy(2 + i).wait_recv()
        far_copy(i).wait_recv()
        part = part + take_near[2 + i] + take_far[i]

        @pl.when(x == y)
        def _():
            final[i] = part

        @pl.when(x != y)
        def _():
            own[14 + i] = part
            swap_copy(i).start()

    def produce(i, carry):
        @pl.when(i < 16)
        def _():
            keep_side = i // 8
            k = (i % 8) // 2
            pair = i % 2
            y_to = keep_side * x + (1 - keep_side) * (1 - x)
            z_to = 2 * ((z_hi + 1 + k) % 2) + (z_lo + 1 + k // 2) % 2
            store_unit(give, i, table_at(y_to, z_to, 1 - core, pair))
            core_copy(i).start()
            store_unit(own, i, table_at(y_to, z_to, core, pair))

        @pl.when((i >= 1) & (i <= 8))
        def _():
            core_copy(i - 1).wait_recv()
            own[i - 1] = own[i - 1] + take_core[i - 1]
            x_copy(i - 1).start()

        for step in range(3):
            @pl.when(i == 2 * step + 1)
            def _():
                moment_copy(step).wait_recv()
                mom_out[step + 1] = mom_out[step] + mom_in[step]
                moment_copy(step + 1).start()

        @pl.when((i >= 9) & (i <= 12))
        def _():
            own[i - 1] = meet(i - 9)
            near_copy(i - 9).start()

        @pl.when((i >= 13) & (i <= 14))
        def _():
            part = meet(i - 9)
            near_copy(i - 13).wait_recv()
            own[i - 1] = part + take_near[i - 13]
            far_copy(i - 13).start()

        @pl.when(i == 15)
        def _():
            close(0)

        return carry

    lax.fori_loop(0, panel_ref.shape[0], fetched, 0)
    lax.fori_loop(0, 16, produce, 0)
    close(1)
    moment_copy(3).wait_recv()
    moments = mom_out[3] + mom_in[3]
    r = lax.broadcasted_iota(jnp.int32, (covs, width), 0)
    c = lax.broadcasted_iota(jnp.int32, (covs, width), 1)
    work = jnp.where(c <= covs, moments, jnp.where(c == r + 64, 1.0, 0.0))
    for k in range(covs):
        scale = 1.0 / jnp.sqrt(work[k : k + 1, k : k + 1])
        pivot = work[k : k + 1, :] * scale
        below = work[:, k : k + 1] * scale
        work = jnp.where(r > k, work - below * pivot, jnp.where(r == k, pivot, work))
    solved_ref[...] = work
    half_score = solved_ref[:, covs : covs + 1]
    inverse = solved_ref[:, 64 : 64 + covs]
    weight_copy.wait()
    gene_copy.wait()
    owner_base = (y * 4 + z) * GENES_OWN
    slot_base = x * 64 + (y * 4 + z) * 8 + core * 4
    squares, sums, traces = [], [], []
    labels = []
    for i in range(2):
        @pl.when(x != y)
        def _():
            swap_copy(i).wait_recv()

        packed = final[i, 0:width]
        mirrored = jnp.transpose(packed)
        last = final[i, width + 2 * covs : UNIT]
        gram_b = jnp.where(row > col, packed, jnp.where(row == col, last[2:3], mirrored))
        grams = (jnp.where(row <= col, packed, mirrored), gram_b)
        for half in range(2):
            cross = final[i, width + half * covs : width + (half + 1) * covs]
            solved = jnp.dot(
                inverse, cross, precision=lax.Precision.HIGHEST,
                preferred_element_type=jnp.float32,
            )
            projected = lax.dot_general(
                solved, solved, (((0,), (0,)), ((), ())), precision=lax.Precision.HIGHEST,
                preferred_element_type=jnp.float32,
            )
            bucket = order_ref[slot_base + 2 * i + half] + x * 64
            label = gene_ref[bucket]
            live = jnp.where(label >= 0, weight_ref[bucket], 0.0)
            across = jnp.broadcast_to(live, (width, width))
            tile = across * jnp.transpose(across) * (grams[half] - projected) / sample_total
            tile_ref[0, 2 * i + half] = tile
            score = last[half : half + 1] - jnp.sum(solved * half_score, axis=0, keepdims=True)
            zscore = live * score / math.sqrt(sample_total)
            squares.append(zscore * zscore)
            sums.append(zscore)
            traces.append(jnp.sum(jnp.where(row == col, tile, 0.0), axis=0, keepdims=True))
            labels.append(label - owner_base)

    gene_row = lax.broadcasted_iota(jnp.int32, (GENES_OWN, width), 0)
    gene_col = lax.broadcasted_iota(jnp.int32, (GENES_OWN, width), 1)
    for n, group in enumerate((squares, sums, traces)):
        total = jnp.zeros((GENES_OWN, width), jnp.float32)
        for label, value in zip(labels, group):
            total = total + jnp.where(label == gene_row, value, 0.0)
        stats[s, n * GENES_OWN : (n + 1) * GENES_OWN] = total

    def stat_copy(n):
        peer = (to_core, to_x, to_corner)[n]
        return remote(stats.at[s], stats.at[s], stat_send.at[n], stat_recv.at[n], peer)

    for n in range(3):
        stat_copy(n).start()
    for n in range(3):
        stat_copy(n).wait_recv()

    def gene_totals(n):
        at = slice(n * GENES_OWN, (n + 1) * GENES_OWN)
        lanes = (stats[0, at] + stats[1, at]) + (stats[2, at] + stats[3, at])
        total = jnp.sum(lanes, axis=1, keepdims=True)
        return jnp.sum(jnp.where(gene_row == gene_col, total, 0.0), axis=0, keepdims=True)

    square, burden, trace = gene_totals(0), gene_totals(1), gene_totals(2)
    rho = jnp.zeros((len(RHO_GRID), width), jnp.float32)
    for n, value in enumerate(RHO_GRID):
        rho = jnp.where(gene_row == n, value, rho)
    rho_all = ((1.0 - rho) * square + rho * (burden * burden)) / width
    rho_ref[...] = rho_all[:, :GENES_OWN]
    trace_ref[...] = trace[:, :GENES_OWN] / width

    def sent_core(i, carry):
        core_copy(i).wait_send()
        return carry

    lax.fori_loop(0, 16, sent_core, 0)

    def sent_x(i, carry):
        x_copy(i).wait_send()
        return carry

    lax.fori_loop(0, 8, sent_x, 0)
    for i in range(4):
        near_copy(i).wait_send()
        moment_copy(i).wait_send()
    for i in range(3):
        stat_copy(i).wait_send()
    for i in range(2):
        far_copy(i).wait_send()

        @pl.when(x != y)
        def _():
            swap_copy(i).wait_send()


def bucket_order(bucket_owner, gene_count, owner_count):
    total = bucket_owner.shape[0]
    bucket = jnp.arange(total, dtype=jnp.int32)
    block = bucket // (total // gene_count)
    label = block * owner_count + bucket_owner
    before = (label[:, None] == label[None, :]) & (bucket[None, :] < bucket[:, None])
    rank = jnp.sum(before.astype(jnp.int32), axis=1)
    place = label * (total // (gene_count * owner_count)) + rank
    inside = bucket % (total // gene_count)
    return jnp.sum(jnp.where(place[None, :] == bucket[:, None], inside[None, :], 0), axis=1)


def shards_fused(
    dosage, covariates, phenotype, sample_mask, variant_weight, bucket_owner, variant_gene
):
    width = BUCKET_WIDTH
    rows, covs = covariates.shape
    total = bucket_owner.shape[0]
    sample_total = rows * lax.axis_size("sample") * lax.axis_size("cohort")
    order = bucket_order(bucket_owner, 2, 8)
    vmem = pl.BlockSpec(memory_space=pltpu.VMEM)
    hbm = pl.BlockSpec(memory_space=pltpu.HBM)

    def units(count):
        return pltpu.VMEM((count, UNIT, width), jnp.float32)

    counts = (16, 16, 8, 8, 4, 4, 2, 2, 2, 2, 4, 4, 3, 3)
    counts = counts + (dosage.shape[1] // width, 2)
    sems = [pltpu.SemaphoreType.DMA((count,)) for count in counts]
    tiles, rho_stats, gene_trace = pl.pallas_call(
        functools.partial(window_kernel, covs, sample_total),
        out_shape=(
            jax.ShapeDtypeStruct((1, 4, width, width), jnp.float32),
            jax.ShapeDtypeStruct((len(RHO_GRID), GENES_OWN), jnp.float32),
            jax.ShapeDtypeStruct((1, GENES_OWN), jnp.float32),
        ),
        in_specs=[pl.BlockSpec(memory_space=pltpu.SMEM), hbm, vmem, vmem, vmem, hbm, hbm],
        out_specs=(vmem, vmem, vmem),
        scratch_shapes=[
            pltpu.VMEM((total, 1, width), jnp.float32),
            pltpu.VMEM((total, 1, width), jnp.int32),
            pltpu.VMEM((dosage.shape[1] // width, rows, width), jnp.bfloat16),
            pltpu.VMEM((48, rows), jnp.bfloat16),
            pltpu.VMEM((width, rows), jnp.bfloat16),
            pltpu.VMEM((covs, width), jnp.float32),
            units(16), units(16), units(16), units(8), units(4), units(2), units(2),
            pltpu.VMEM((4, covs, width), jnp.float32),
            pltpu.VMEM((4, covs, width), jnp.float32),
            pltpu.VMEM((4, 3 * GENES_OWN, width), jnp.float32),
        ] + sems,
        compiler_params=pltpu.CompilerParams(
            collective_id=0, has_side_effects=True, vmem_limit_bytes=62 * 1024 * 1024
        ),
        cost_estimate=pl.CostEstimate(
            flops=2 * rows * width * 176 * 64, bytes_accessed=2 * dosage.size, transcendentals=0
        ),
    )(
        order, dosage, covariates.T, phenotype.reshape(1, rows), sample_mask.reshape(1, rows),
        variant_weight.reshape(total, 1, width), variant_gene.reshape(total, 1, width),
    )
    return tiles, rho_stats, gene_trace.reshape(GENES_OWN)


def solution(mesh):
    placed = (
        P(("sample", "cohort"), "gene"),
        P(("sample", "cohort"), None),
        P(("sample", "cohort")),
        P(("sample", "cohort")),
        P(),
        P(),
        P(),
    )
    shape = dict(mesh.shape)
    fused = (shape["sample"], shape["gene"], shape["cohort"]) == (4, 2, 4)
    body = shards_fused if fused else shards
    return jax.shard_map(
        body,
        mesh=mesh,
        in_specs=placed,
        out_specs=(
            P(("gene", "cohort"), "sample", None, None),
            P(None, ("gene", "cohort")),
            P(("gene", "cohort")),
        ),
        check_vma=False,
    )
```
